32 devices in a mesh: dp: 16 (over z, y, core), head: 2 (over x).
Axes of the slice: x: 2, y: 2, z: 4, core: 2. Of those that a mesh axis runs over, the one named last changes fastest.
Arguments:
- tokens: bfloat16 [16384, 1024], P(('dp', 'head')), may hold values from -6 to 6
- seq_lengths: int32 [16, 2], P('dp'), may hold values from 128 to 896, as said below
- pass_embed: float32 [1024], replicated, may hold values from -3 to 3
- norm1_gain: float32 [1024], replicated, may hold values from 0.1 to 1.9
- qkv_weight: bfloat16 [1024, 3072], replicated, may hold values from -0.1875 to 0.1875
- out_weight: bfloat16 [1024, 1024], replicated, may hold values from -0.75 to 0.75
- norm2_gain: float32 [1024], replicated, may hold values from 0.1 to 1.9
- up_weight: bfloat16 [1024, 4096], replicated, may hold values from -0.1875 to 0.1875
- down_weight: bfloat16 [4096, 1024], replicated, may hold values from -0.09375 to 0.09375
- cotangent: bfloat16 [16384, 1024], P(('dp', 'head')), may hold values from -6 to 6
Outputs:
- mixed: bfloat16 [16384, 1024], P(('dp', 'head'))
- token_grad: bfloat16 [16384, 1024], P(('dp', 'head'))
- pass_grad: float32 [1024], P(('dp', 'head'))
- norm1_grad: float32 [1024], P(('dp', 'head'))
- qkv_grad: float32 [1024, 3072], P(('dp', 'head'))
- out_grad: float32 [1024, 1024], P(('dp', 'head'))
- norm2_grad: float32 [1024], P(('dp', 'head'))
- up_grad: float32 [1024, 4096], P(('dp', 'head'))
- down_grad: float32 [4096, 1024], P(('dp', 'head'))
The draws below stay inside these ranges and needn't reach their ends.
Inputs may be any that keep to these rules, and one draw needn't show every extreme that they name: `seq_lengths`: each row sums to 1024; in each row one length is under 512 and the other is the rest of the group; some row holds exactly 896.
All inputs are finite; a program needn't handle non-finite values.
Results may differ from the reference program's by a relative error of at most 0.009.
Values may be sent and summed in bfloat16 or wider, within the bound.
No kernel may reach another device: no remote copies, remote signals or barrier semaphores. Data moves between devices by JAX's collectives and lax.ppermute only.
A program may use at most 320 MiB of HBM per device.

```python
import jax
import jax.numpy as jnp
from jax import lax

D = 1024
HEADS = 16
HEAD_DIM = 64
FF = 4096
TOK_DEV = 512
GROUP_ROWS = 1024
MIN_SEQ = 128
TOKENS = 16384
N_DP = 16
N_HEAD = 2


def draw_seq_lengths(key, part):
    key = jax.random.fold_in(key, 7)
    key_len, key_pick, key_flip = jax.random.split(key, 3)
    short = jax.random.randint(key_len, (N_DP,), MIN_SEQ, TOK_DEV).astype(jnp.int32)
    chosen = jax.random.randint(key_pick, (), 0, N_DP).astype(jnp.int32)
    short = jnp.where(jnp.arange(N_DP, dtype=jnp.int32) == chosen, MIN_SEQ, short).astype(jnp.int32)
    longer = (GROUP_ROWS - short).astype(jnp.int32)
    flipped = jax.random.randint(key_flip, (N_DP,), 0, 2).astype(jnp.int32)
    leading = jnp.where(flipped == 1, short, longer)
    trailing = jnp.where(flipped == 1, longer, short)
    return jnp.stack([leading, trailing], axis=1).astype(jnp.int32)


def level_of(own_key, extent, cuts, low, top_value):
    loudness, own = 1.0, jax.random.fold_in(own_key, 6)
    for axis_at, shards_of in cuts:
        heights = jnp.exp(jax.random.uniform(jax.random.fold_in(own, axis_at), (shards_of,), jnp.float32, low / len(cuts), top_value / len(cuts)))
        loudness = loudness * jnp.repeat(heights, extent[axis_at] // shards_of).reshape([-1 if axis == axis_at else 1 for axis in range(len(extent))])
    return loudness


def normal_values(key, extent, spread, most, cuts=(), kind=jnp.bfloat16):
    result = spread * jax.random.normal(key, extent, jnp.float32)
    if cuts:
        result = result * level_of(key, extent, cuts, -0.22, 0.18)
    return jnp.clip(result, -most, most).astype(kind)


def setup_inputs(seed: int = 0) -> dict:
    key_of = jax.random.split(jax.random.key(seed), 11)
    return {
        "tokens": normal_values(key_of[0], (TOKENS, D), 1.0, 6.0, ((0, 32),)),
        "seq_lengths": draw_seq_lengths(jax.random.fold_in(key_of[10], 71), 0),
        "pass_embed": normal_values(key_of[2], (D,), 0.5, 3.0, (), jnp.float32),
        "norm1_gain": jnp.clip(1.0 + 0.18 * jax.random.normal(key_of[3], (D,), jnp.float32), 0.1, 1.9),
        "qkv_weight": normal_values(key_of[4], (D, 3 * D), D ** -0.5, 0.1875),
        "out_weight": normal_values(key_of[5], (D, D), (D // 16) ** -0.5, 0.75),
        "norm2_gain": jnp.clip(1.0 + 0.18 * jax.random.normal(key_of[6], (D,), jnp.float32), 0.1, 1.9),
        "up_weight": normal_values(key_of[7], (D, FF), D ** -0.5, 0.1875),
        "down_weight": normal_values(key_of[8], (FF, D), FF ** -0.5, 0.09375),
        "cotangent": normal_values(key_of[9], (TOKENS, D), 1.0, 6.0, ((0, 32),)),
    }


precise = lax.Precision.HIGHEST

@jax.custom_vjp
def low(v):
    return lax.optimization_barrier(v.astype(jnp.bfloat16)).astype(jnp.float32)

@jax.custom_vjp
def low_back(v):
    return v

def low_keep(v):
    return (low(v), None)

def low_pass(kept, grad):
    return (grad,)

def back_keep(v):
    return (v, None)

def back_low(kept, grad):
    return (low(grad),)
low.defvjp(low_keep, low_pass)
low_back.defvjp(back_keep, back_low)

def layer_norm(hidden, gain):
    row_mean = lax.optimization_barrier(jnp.mean(hidden, axis=-1, keepdims=True))
    centred = hidden - row_mean
    variance = lax.optimization_barrier(jnp.mean(centred * centred, axis=-1, keepdims=True))
    return centred * lax.rsqrt(variance + 1e-05) * gain

def segment_ids(lengths, group_rows):
    seq_ends = jnp.cumsum(lengths).astype(jnp.int32)
    positions = jnp.arange(group_rows, dtype=jnp.int32)
    return lax.optimization_barrier(jnp.sum((positions[:, None] >= seq_ends[None, :]).astype(jnp.int32), axis=1)).astype(jnp.int32)

def attention_all(query, key, value, segment):
    group_rows = query.shape[0]
    block_rows = min(512, group_rows)
    positions = jnp.arange(group_rows, dtype=jnp.int32)

    def one_block(index):
        start = (index * block_rows).astype(jnp.int32)
        query_block = lax.dynamic_slice_in_dim(query, start, block_rows, 0)
        rows_here = start + jnp.arange(block_rows, dtype=jnp.int32)
        seg_here = lax.dynamic_slice_in_dim(segment, start, block_rows, 0)
        scores = low_back(jnp.einsum('bhd,ehd->hbe', query_block, key, precision=precise) * HEAD_DIM ** (-0.5))
        allowed = (seg_here[:, None] == segment[None, :]) & (positions[None, :] <= rows_here[:, None])
        scores = jnp.where(allowed[None], scores, -1e+30)
        attn_probs = low(jax.nn.softmax(scores, axis=-1))
        return jnp.einsum('hbe,ehd->bhd', attn_probs, value, precision=precise)
    blocks = lax.map(jax.checkpoint(one_block), jnp.arange(group_rows // block_rows, dtype=jnp.int32))
    return blocks.reshape(group_rows, HEADS * HEAD_DIM)

def layer_forward(tokens, segment, pass_embed, norm1_gain, qkv_weight, out_weight, norm2_gain, up_weight, down_weight):
    group_rows = tokens.shape[0]
    resid = tokens + pass_embed
    normed_a = low(layer_norm(resid, norm1_gain))
    projected = low_back(low(jnp.dot(normed_a, qkv_weight, precision=precise)))
    split_heads = projected.reshape(group_rows, 3, HEADS, HEAD_DIM)
    attended = low_back(low(attention_all(split_heads[:, 0], split_heads[:, 1], split_heads[:, 2], segment)))
    middle = resid + low_back(jnp.dot(attended, out_weight, precision=precise))
    normed_m = low(layer_norm(middle, norm2_gain))
    upper = low_back(jnp.dot(normed_m, up_weight, precision=precise))
    active = low(jax.nn.gelu(upper, approximate=True))
    return middle + jnp.dot(active, down_weight, precision=precise)

def reference(tokens, seq_lengths, pass_embed, norm1_gain, qkv_weight, out_weight, norm2_gain, up_weight, down_weight, cotangent):
    group_rows = TOK_DEV * N_HEAD
    params = tuple((arr.astype(jnp.float32) for arr in (pass_embed, norm1_gain, qkv_weight, out_weight, norm2_gain, up_weight, down_weight)))
    inputs = tokens.reshape(N_DP, group_rows, D).astype(jnp.float32)
    cotans = cotangent.reshape(N_DP, group_rows, D).astype(jnp.float32)

    def one_group(scan_state, group_item):
        group_tokens, group_cot, group_lengths = group_item
        segment = segment_ids(group_lengths, group_rows)

        def forward(group_in, *weights):
            return layer_forward(group_in, segment, *weights)
        output, pullback = jax.vjp(forward, group_tokens, *params)
        grads = pullback(group_cot)
        scan_state = tuple((total + grad_term for total, grad_term in zip(scan_state, grads[1:])))
        return (scan_state, (output.astype(jnp.bfloat16), grads[0].astype(jnp.bfloat16)))
    zeros_init = tuple((jnp.zeros(arr.shape, jnp.float32) for arr in params))
    sums, (outputs, token_grads) = lax.scan(one_group, zeros_init, (inputs, cotans, seq_lengths))
    return (outputs.reshape(N_DP * group_rows, D), token_grads.reshape(N_DP * group_rows, D), sums[0], sums[1], sums[2], sums[3], sums[4], sums[5], sums[6])
```

```python
from functools import partial

import jax
import jax.numpy as jnp
from jax import lax
from jax.sharding import Mesh, PartitionSpec as P

HEADS = 16
HEAD_DIM = 64
AXES = ("chip", "core", "half", "lane")
F32 = jnp.float32
BF16 = jnp.bfloat16


def layer_norm(hidden, gain):
    row_mean = jnp.mean(hidden, axis=-1, keepdims=True)
    centred = hidden - row_mean
    variance = jnp.mean(centred * centred, axis=-1, keepdims=True)
    return centred * lax.rsqrt(variance + 1e-05) * gain


def layer_norm_back(hidden, gain, incoming):
    row_mean = jnp.mean(hidden, axis=-1, keepdims=True)
    centred = hidden - row_mean
    variance = jnp.mean(centred * centred, axis=-1, keepdims=True)
    scale = lax.rsqrt(variance + 1e-05)
    x_hat = centred * scale
    gain_terms = incoming * x_hat
    scaled = incoming * gain
    mean_a = jnp.mean(scaled, axis=-1, keepdims=True)
    mean_b = jnp.mean(scaled * x_hat, axis=-1, keepdims=True)
    return scale * (scaled - mean_a - x_hat * mean_b), jnp.sum(gain_terms, axis=0)


def dot(a, b, ca=1, cb=0):
    return lax.dot_general(a, b, (((ca,), (cb,)), ((), ())), preferred_element_type=F32)


def body(
    sizes,
    tokens,
    seq_lengths,
    pass_embed,
    norm1_gain,
    qkv_weight,
    out_weight,
    norm2_gain,
    up_weight,
    down_weight,
    cotangent,
):
    n_chip, n_core, n_half, n_lane = sizes
    n_head = n_half * n_lane
    tok_rows, width = tokens.shape
    rows = 2 * tok_rows
    group_rows = tok_rows * n_head
    hidden = up_weight.shape[1]
    core = lax.axis_index("core")
    chip = lax.axis_index("chip")
    head = lax.axis_index("half") * n_lane + lax.axis_index("lane")

    def index(c, k, h, l):
        return ((c * n_core + k) * n_half + h) * n_lane + l

    everyone = [
        (c, k, h, l)
        for c in range(n_chip)
        for k in range(n_core)
        for h in range(n_half)
        for l in range(n_lane)
    ]
    regroup_perm = [(index(c, k, h, l), index(c, h, k, l)) for c, k, h, l in everyone]

    def regroup(value):
        return lax.ppermute(value, AXES, regroup_perm)

    def across(value):
        return lax.ppermute(value, "core", [(0, 1), (1, 0)])

    def in_order(own, other, axis):
        return jnp.where(
            core == 0,
            jnp.concatenate([own, other], axis=axis),
            jnp.concatenate([other, own], axis=axis),
        )

    n_bits = (n_chip * n_head).bit_length() - 1

    def flip(order, step):
        def partner(c, k, h, l):
            number = (c * n_head + h * n_lane + l) ^ (1 << order[k][step])
            return index(
                number // n_head, k, number % n_head // n_lane, number % n_lane
            )

        return [(index(*d), partner(*d)) for d in everyone]

    number = chip * n_head + head

    def scatter_sum(blocks, first, second):
        rest = [b for b in range(n_bits) if b not in (first, second)]
        order = ([first, second, *rest], [second, first, *rest])
        view = blocks.reshape((2,) * n_bits + blocks.shape[1:])
        tail = tuple(range(n_bits, view.ndim))
        front = [
            jnp.transpose(view, tuple(n_bits - 1 - b for b in o) + tail) for o in order
        ]
        parts = [jnp.where(core == 0, front[0], front[1])]
        for step in range(n_bits):
            mine = jnp.where(
                core == 0,
                (number >> order[0][step]) & 1,
                (number >> order[1][step]) & 1,
            )

            def take(part, at):
                return lax.dynamic_index_in_dim(part, at, 0, keepdims=False)

            gone = sum(take(p, 1 - mine).astype(F32) for p in parts).astype(BF16)
            came = lax.ppermute(gone, AXES, flip(order, step))
            parts = [take(p, mine) for p in parts] + [came]
        return sum(p.astype(F32) for p in parts)

    def by_chip_rows(grad):
        per = width // (n_chip * n_core * n_head)
        view = grad.reshape(n_chip, n_core, n_head, per, grad.shape[1])
        return jnp.swapaxes(view, 1, 2).reshape(
            n_chip * n_head, n_core, per, grad.shape[1]
        )

    def finish_rows(block, interleave):
        own = lax.dynamic_index_in_dim(block, core, 0, keepdims=False)
        gone = lax.dynamic_index_in_dim(block, 1 - core, 0, keepdims=False)
        came = across(gone)
        per = own.shape[0]
        own = own.reshape(per, -1, interleave)
        came = came.reshape(per, -1, interleave)
        pair = jnp.stack(
            [jnp.where(core == 0, own, came), jnp.where(core == 0, came, own)], axis=2
        )
        return pair.reshape(per, -1)

    own_tokens = regroup(tokens)
    own_lengths = regroup(seq_lengths)
    own_cot = regroup(cotangent)
    toks = in_order(own_tokens, across(own_tokens), 0)
    cot = in_order(own_cot, across(own_cot), 0)

    ff_block = hidden // (n_chip * n_core)
    up_here = lax.dynamic_index_in_dim(
        up_weight.reshape(width, n_chip, n_core, ff_block), core, 2, keepdims=False
    ).reshape(width, hidden // 2)
    down_here = lax.dynamic_index_in_dim(
        down_weight.reshape(n_chip, n_core, ff_block, width), core, 1, keepdims=False
    ).reshape(hidden // 2, width)
    qkv_here = lax.dynamic_index_in_dim(
        qkv_weight.reshape(width, 3, n_core, width // 2), core, 2, keepdims=False
    ).reshape(width, 3 * width // 2)
    out_here = lax.dynamic_slice_in_dim(out_weight, core * (width // 2), width // 2, 0)

    resid = toks.astype(F32) + pass_embed
    normed_a = layer_norm(resid, norm1_gain).astype(BF16)
    qkv = dot(normed_a, qkv_here).astype(BF16)

    heads_core = HEADS // 2
    heads_here = heads_core // n_lane

    def to_heads(value, many):
        value = value.reshape(rows, many, heads_core, HEAD_DIM)
        if n_lane > 1:
            value = lax.all_to_all(value, "lane", split_axis=2, concat_axis=0, tiled=True)
            value = jnp.swapaxes(
                value.reshape(n_lane, 2, tok_rows, many, heads_here, HEAD_DIM), 0, 1
            ).reshape(group_rows, many, heads_here, HEAD_DIM)
        return value

    def from_heads(value, many):
        if n_lane > 1:
            value = jnp.swapaxes(
                value.reshape(2, n_lane, tok_rows, many, heads_here, HEAD_DIM), 0, 1
            ).reshape(group_rows, many, heads_here, HEAD_DIM)
            value = lax.all_to_all(value, "lane", split_axis=0, concat_axis=2, tiled=True)
        return value.reshape(rows, many * width // 2)

    headwise = to_heads(qkv, 3)
    query, key, value = headwise[:, 0], headwise[:, 1], headwise[:, 2]
    lengths = own_lengths[0]
    ends = jnp.sum(
        jnp.where(
            jnp.arange(lengths.shape[0])[:, None] <= jnp.arange(lengths.shape[0])[None, :],
            lengths[:, None],
            0,
        ),
        axis=0,
    )
    positions = jnp.arange(group_rows, dtype=jnp.int32)
    segment = jnp.sum((positions[:, None] >= ends[None, :]).astype(jnp.int32), axis=1)
    block_rows = min(512, group_rows)
    block_count = group_rows // block_rows
    score_scale = HEAD_DIM ** (-0.5)

    def block_scores(at):
        start = at * block_rows
        end_row = start + block_rows
        scores = (
            jnp.einsum(
                "bhd,ehd->hbe", query[start:end_row], key[:end_row], preferred_element_type=F32
            )
            * score_scale
        )
        allowed = (segment[start:end_row, None] == segment[None, :end_row]) & (
            positions[None, :end_row] <= positions[start:end_row, None]
        )
        return jnp.where(allowed[None], scores, -1e30)

    attended_parts = []
    log_totals = []
    for at in range(block_count):
        end_row = (at + 1) * block_rows
        scores = block_scores(at)
        row_max = jnp.max(scores, axis=-1, keepdims=True)
        exp_scores = jnp.exp(scores - row_max)
        row_total = jnp.sum(exp_scores, axis=-1, keepdims=True)
        attn_probs = (exp_scores / row_total).astype(BF16)
        log_totals.append(row_max + jnp.log(row_total))
        attended_parts.append(
            jnp.einsum(
                "hbe,ehd->bhd", attn_probs, value[:end_row], preferred_element_type=F32
            ).astype(BF16)
        )
    attended_heads = jnp.concatenate(attended_parts, axis=0)
    attended_here = from_heads(attended_heads[:, None], 1)
    attended = in_order(attended_here, across(attended_here), 1)

    middle = resid + dot(attended, out_weight)
    normed_m = layer_norm(middle, norm2_gain).astype(BF16)
    upper = dot(normed_m, up_here)
    gelu_tanh = partial(jax.nn.gelu, approximate=True)
    active = gelu_tanh(upper).astype(BF16)
    active_grad = dot(cot, down_here, 1, 1)
    _, gelu_pull = jax.vjp(gelu_tanh, upper)
    upper_grad = gelu_pull(active_grad)[0].astype(BF16)

    down_part = dot(active, cot, 0, 0).astype(BF16)
    per_ff = hidden // (n_chip * n_core * n_head)
    down_grad = scatter_sum(down_part.reshape(n_chip * n_head, per_ff, width), 0, 1)
    up_part = dot(normed_m, upper_grad, 0, 0).astype(BF16)
    up_block = scatter_sum(by_chip_rows(up_part), 1, 0)
    up_grad = finish_rows(up_block, ff_block)

    normed_m_part = dot(upper_grad, up_here, 1, 1).astype(BF16)
    normed_m_grad = normed_m_part.astype(F32) + across(normed_m_part).astype(F32)
    middle_part, norm2_terms = layer_norm_back(middle, norm2_gain, normed_m_grad)
    norm2_terms = norm2_terms * 0.5
    middle_grad = cot.astype(F32) + middle_part
    branch_grad = middle_grad.astype(BF16)

    output_part = dot(active, down_here)

    def rows_of(value, which):
        return lax.dynamic_slice_in_dim(value, which * tok_rows, tok_rows, 0)

    output_came = across(rows_of(output_part, 1 - core).astype(BF16))
    mixed = (rows_of(middle, core) + rows_of(output_part, core) + output_came.astype(F32)).astype(BF16)
    mixed = regroup(mixed)

    branch_cols = lax.dynamic_slice_in_dim(branch_grad, core * (width // 2), width // 2, 1)
    out_part = dot(attended, branch_cols, 0, 0).astype(BF16)
    attended_grad = dot(branch_grad, out_here, 1, 1).astype(BF16)
    attended_grad = to_heads(attended_grad, 1)[:, 0]

    key_grad = jnp.zeros((group_rows, heads_here, HEAD_DIM), F32)
    value_grad = jnp.zeros((group_rows, heads_here, HEAD_DIM), F32)
    query_parts = []
    for at in range(block_count):
        start = at * block_rows
        end_row = start + block_rows
        scores = block_scores(at)
        attn_probs = jnp.exp(scores - log_totals[at])
        probs_low = attn_probs.astype(BF16)
        out_block_grad = attended_grad[start:end_row]
        value_grad = value_grad.at[:end_row].add(
            jnp.einsum("hbe,bhd->ehd", probs_low, out_block_grad, preferred_element_type=F32)
        )
        prob_grad = jnp.einsum(
            "bhd,ehd->hbe", out_block_grad, value[:end_row], preferred_element_type=F32
        )
        row_delta = jnp.sum(attn_probs * prob_grad, axis=-1, keepdims=True)
        score_grad = (attn_probs * (prob_grad - row_delta)).astype(BF16)
        query_parts.append(
            jnp.einsum("hbe,ehd->bhd", score_grad, key[:end_row], preferred_element_type=F32)
            * score_scale
        )
        key_grad = key_grad.at[:end_row].add(
            jnp.einsum("hbe,bhd->ehd", score_grad, query[start:end_row], preferred_element_type=F32)
            * score_scale
        )
    query_grad = jnp.concatenate(query_parts, axis=0)
    qkv_back = from_heads(
        jnp.stack([query_grad, key_grad, value_grad], axis=1).astype(BF16), 3
    )

    normed_a_part = dot(qkv_back, qkv_here, 1, 1)
    normed_a_came = across(rows_of(normed_a_part, 1 - core).astype(BF16))
    normed_a_grad = rows_of(normed_a_part, core) + normed_a_came.astype(F32)
    qkv_part = dot(normed_a, qkv_back, 0, 0).astype(BF16)
    rest_part = jnp.concatenate([out_part, qkv_part], axis=1)
    rest_block = scatter_sum(by_chip_rows(rest_part), 0, 1)
    rest = finish_rows(rest_block, width // 2)
    out_grad, qkv_grad = rest[:, :width], rest[:, width:]

    resid_part, norm1_terms = layer_norm_back(rows_of(resid, core), norm1_gain, normed_a_grad)
    resid_grad = rows_of(middle_grad, core) + resid_part
    token_grad = regroup(resid_grad.astype(BF16))
    pass_terms = jnp.sum(resid_grad, axis=0)
    small = jnp.stack([pass_terms, norm1_terms, norm2_terms])
    n_all = len(everyone)
    small = jnp.swapaxes(small.reshape(3, n_all, width // n_all), 0, 1)
    small = lax.all_to_all(small, AXES, split_axis=0, concat_axis=0, tiled=True)
    small = jnp.sum(small, axis=0)
    return (
        mixed,
        token_grad,
        small[0],
        small[1],
        qkv_grad,
        out_grad,
        small[2],
        up_grad,
        down_grad,
    )


def solution(mesh):
    n_dp, n_head = mesh.shape["dp"], mesh.shape["head"]
    sizes = (n_dp // 2, 2, 2, n_head // 2)
    fine = Mesh(mesh.devices.reshape(sizes), AXES)
    rows, group = P(AXES), P(("chip", "core"))
    in_specs = (rows, group, P(), P(), P(), P(), P(), P(), P(), rows)
    return jax.shard_map(
        partial(body, sizes),
        mesh=fine,
        in_specs=in_specs,
        out_specs=(rows,) * 9,
        check_vma=False,
    )
```

```python
from functools import partial

import jax
import jax.numpy as jnp
from jax import lax
from jax.experimental import pallas as pl
from jax.experimental.pallas import tpu as pltpu
from jax.sharding import Mesh, PartitionSpec as P

HEADS = 16
HEAD_DIM = 64
AXES = ("chip", "core", "half", "lane")
F32 = jnp.float32
BF16 = jnp.bfloat16
COST = 20
SCORE_SCALE = HEAD_DIM**-0.5 * 1.4426950408889634
GELU_A, GELU_B = 0.7978845608028654, 0.044715


def call(kernel, scalars, inputs, in_blocks, out_shapes, out_blocks, grid, scratch=(), flops=0, aliases=None):
    (steps,) = grid
    scalars, line = scalars
    n_in, n_out, body = len(inputs), len(out_shapes), kernel
    inputs, in_blocks = [*inputs, *line["turn"]], [*in_blocks, *["any"] * len(line["turn"])]
    out_shapes, out_blocks = [*out_shapes, sds((8, 128), F32)], [*out_blocks, "any"]
    first_in, first_out = len(inputs), n_out + 1
    riders, widths = line["riders"], []
    line["riders"] = []
    base = scalars.shape[0]
    for rider in riders:
        starts, parts, count = rider["next_step"]()
        tail = parts[0].shape[1:]
        zeros = (0,) * len(tail)
        per = count // steps if count % steps == 0 else 1
        blocks = count // per
        for k, part in enumerate(parts):
            inputs.append(part)
            in_blocks.append(
                (
                    (per, *tail),
                    lambda g, s, at=base + k, b=blocks, z=zeros: (
                        s[at] * b + jnp.minimum(g, b - 1),
                        *z,
                    ),
                )
            )
        out_shapes.append(sds((count, *tail), BF16))
        out_blocks.append(
            ((per, *tail), lambda g, s, b=blocks, z=zeros: (jnp.minimum(g, b - 1), *z))
        )
        scalars = jnp.concatenate([scalars, starts])
        base += len(parts)
        widths.append(len(parts))

    def kernel(scalars_ref, *refs):
        ins, outs = refs[: len(inputs)], refs[len(inputs) : len(inputs) + len(out_shapes)]
        rest = refs[len(inputs) + len(out_shapes) :]
        body(scalars_ref, *ins[:n_in], *outs[:n_out], *rest)
        at = first_in
        for n, width in enumerate(widths):
            outs[first_out + n][...] = sum(
                r[...].astype(F32) for r in ins[at : at + width]
            ).astype(BF16)
            at += width

    def spec(array, block):
        if block is None:
            rank = len(array.shape)
            return pl.BlockSpec(array.shape, lambda *_: (0,) * rank)
        if block == "any":
            return pl.BlockSpec(memory_space=pl.ANY)
        return pl.BlockSpec(*block)

    moved = sum(a.size * a.dtype.itemsize for a in (*inputs, *out_shapes))
    outs = pl.pallas_call(
        kernel,
        out_shape=out_shapes,
        grid_spec=pltpu.PrefetchScalarGridSpec(
            num_scalar_prefetch=1,
            grid=grid,
            in_specs=[spec(a, b) for a, b in zip(inputs, in_blocks, strict=True)],
            out_specs=[spec(a, b) for a, b in zip(out_shapes, out_blocks, strict=True)],
            scratch_shapes=list(scratch),
        ),
        compiler_params=pltpu.CompilerParams(vmem_limit_bytes=56 * 2**20),
        cost_estimate=pl.CostEstimate(flops=flops * COST, bytes_accessed=moved * COST, transcendentals=0),
        input_output_aliases=aliases or {},
    )(scalars, *inputs)
    line["turn"] = [outs[n_out]]
    for rider, gone in zip(riders, outs[first_out:]):
        rider["send"](gone)
    return list(outs[:n_out])


def sds(shape, dtype):
    return jax.ShapeDtypeStruct(shape, dtype)


def moments(hidden):
    row_mean = jnp.mean(hidden, axis=-1, keepdims=True)
    centred = hidden - row_mean
    variance = jnp.mean(centred * centred, axis=-1, keepdims=True)
    return centred, lax.rsqrt(variance + 1e-05)


def dot(a, b, ca=1, cb=0):
    return lax.dot_general(a, b, (((ca,), (cb,)), ((), ())), preferred_element_type=F32)


def weights_here(core, up_weight, qkv_weight, block):
    width, hidden = up_weight.shape
    tall, two = 128, 2 * HEAD_DIM
    pairs = width // 2 // two

    def kernel(core_ref, up_ref, qkv_ref, up_out, qkv_out):
        c = core_ref[0]
        for n in range(hidden // 2 // block):
            start = pl.multiple_of((2 * n + c) * block, block)
            up_out[:, n * block : (n + 1) * block] = up_ref[:, pl.ds(start, block)]
        for p in range(pairs):
            for t in range(3):
                start = pl.multiple_of(t * width + c * (width // 2) + p * two, two)
                to = (3 * p + t) * two
                qkv_out[:, to : to + two] = qkv_ref[:, pl.ds(start, two)]

    def by_rows(columns):
        return ((tall, columns), lambda i, c: (i, 0))

    return call(
        kernel,
        core,
        [up_weight, qkv_weight],
        [by_rows(hidden), by_rows(3 * width)],
        [sds((width, hidden // 2), BF16), sds((width, 3 * width // 2), BF16)],
        [by_rows(hidden // 2), by_rows(3 * width // 2)],
        (width // tall,),
    )


def copy_picked(stays, pairs, copy):
    for here, came, row in pairs:
        @pl.when(stays == 1)
        def _():
            copy(here, row)

        @pl.when(stays != 1)
        def _():
            copy(came, row)


def project_qkv(at, pairs, pass_embed, gain, weight, into=None):
    pieces = [p for pair in pairs for p in pair]
    width = pieces[0].shape[1]
    heights = [pair[0].shape[0] for pair in pairs]
    half = sum(heights)
    rows, wide = 2 * half, 512
    columns = weight.shape[1]

    def kernel(at_ref, *refs):
        piece_refs, (pass_ref, gain_ref, w_ref, *refs) = refs[: len(pieces)], refs[len(pieces) :]
        toks_ref, normed_ref, qkv_ref = refs[-3:]

        def norm_rows(ref, row):
            for start in range(0, ref.shape[0], 64):
                low = ref[start : start + 64, :]
                centred, scale = moments(low.astype(F32) + pass_ref[...])
                to = slice(row + start, row + start + 64)
                toks_ref[to, :] = low
                normed_ref[to, :] = (centred * scale * gain_ref[...]).astype(BF16)

        @pl.when(pl.program_id(0) == 0)
        def _():
            firsts = [sum(heights[:n]) for n in range(len(pairs))]
            copy_picked(
                at_ref[1],
                [(piece_refs[2 * n], piece_refs[2 * n + 1], f) for n, f in enumerate(firsts)],
                norm_rows,
            )

        qkv_ref[...] = dot(normed_ref[...], w_ref[...]).astype(BF16)

    inputs = [*pieces, pass_embed, gain, weight]
    in_blocks = [*[None] * (len(pieces) + 2), ((width, wide), lambda j, a: (0, j))]
    aliases = {}
    if into is not None:
        aliases = {len(inputs) + 1 + n: n for n in range(3)}
        inputs += into
        in_blocks += ["any"] * 3
    all_rows = ((half, width), lambda j, a: (a[0], 0))
    return call(
        kernel,
        at,
        inputs,
        in_blocks,
        [sds((rows, width), BF16), sds((rows, width), BF16), sds((rows, columns), BF16)],
        [all_rows, all_rows, ((half, wide), lambda j, a: (a[0], j))],
        (columns // wide,),
        flops=rows * width * columns,
        aliases=aliases,
    )


def allowed(first_key, first_query, keys, queries, ends, diagonal):
    at_query = first_query + lax.broadcasted_iota(jnp.int32, (1, queries), 1)
    start = jnp.zeros_like(at_query)
    for end in ends:
        start = jnp.where(at_query >= end, end, start)
    at_key = first_key + lax.broadcasted_iota(jnp.int32, (keys, queries), 0)
    mask = at_key >= start
    if diagonal:
        mask = mask & (at_key <= at_query)
    return mask


def attention_block(group_rows):
    return 256 if group_rows <= 1024 else 512


def attend(ends, qkv):
    group_rows, columns = qkv.shape
    pairs = columns // (6 * HEAD_DIM)
    step = attention_block(group_rows)
    n_ends = ends[0].shape[0]

    def kernel(ends_ref, qkv_ref, o_ref, total_ref, vt_ref):
        q_ref, k_ref, v_ref = (qkv_ref.at[:, pl.ds(2 * HEAD_DIM * n, 2 * HEAD_DIM)] for n in range(3))
        bounds = [ends_ref[n] for n in range(n_ends)]
        vt_ref[...] = jnp.transpose(v_ref[...])
        lane = lax.broadcasted_iota(jnp.int32, (1, 2 * HEAD_DIM), 1)
        for i in range(group_rows // step):
            rows = slice(i * step, (i + 1) * step)
            outs = []
            masks = [
                allowed(j * step, i * step, step, step, bounds, j == i) for j in range(i + 1)
            ]
            for h in range(2):
                q = jnp.where(lane // HEAD_DIM == h, q_ref[rows, :], 0)
                scores = [
                    jnp.where(
                        masks[j],
                        dot(k_ref[j * step : (j + 1) * step, :], q, 1, 1) * SCORE_SCALE,
                        -1e30,
                    )
                    for j in range(i + 1)
                ]
                top = jnp.max(scores[0], axis=0, keepdims=True)
                for s in scores[1:]:
                    top = jnp.maximum(top, jnp.max(s, axis=0, keepdims=True))
                total = jnp.zeros_like(top)
                out = jnp.zeros((HEAD_DIM, step), F32)
                for j in range(i + 1):
                    p = jnp.exp2(scores[j] - top)
                    total = total + jnp.sum(p, axis=0, keepdims=True)
                    out = out + dot(
                        vt_ref[h * HEAD_DIM : (h + 1) * HEAD_DIM, j * step : (j + 1) * step],
                        p.astype(BF16),
                    )
                outs.append(out * (1.0 / total))
                total_ref[0, h : h + 1, rows] = top + jnp.log2(total)
            o_ref[rows, :] = jnp.transpose(jnp.concatenate(outs, axis=0)).astype(BF16)

    block = (group_rows, 2 * HEAD_DIM)
    return call(
        kernel,
        ends,
        [qkv],
        [((group_rows, 6 * HEAD_DIM), lambda p, e: (0, p))],
        [
            sds((group_rows, pairs * 2 * HEAD_DIM), BF16),
            sds((pairs, 2, group_rows), F32),
        ],
        [(block, lambda p, e: (0, p)), ((1, 2, group_rows), lambda p, e: (p, 0, 0))],
        (pairs,),
        scratch=[pltpu.VMEM((2 * HEAD_DIM, group_rows), BF16)],
        flops=pairs * 4 * group_rows * group_rows * 2 * HEAD_DIM,
    )


def attend_back(ends, qkv, attended, attended_grad, totals, first, pairs):
    group_rows = qkv.shape[0]
    step = attention_block(group_rows)
    n_ends = ends[0].shape[0]

    def kernel(ends_ref, qkv_ref, o_ref, g_ref, total_ref, out_ref, dk_acc, dv_acc):
        q_ref, k_ref, v_ref = (qkv_ref.at[:, pl.ds(2 * HEAD_DIM * n, 2 * HEAD_DIM)] for n in range(3))
        bounds = [ends_ref[n] for n in range(n_ends)]
        lane = lax.broadcasted_iota(jnp.int32, (1, 2 * HEAD_DIM), 1)
        for i in range(group_rows // step):
            rows = slice(i * step, (i + 1) * step)
            products = jnp.transpose(g_ref[rows, :].astype(F32) * o_ref[rows, :].astype(F32))
            masks = [
                allowed(j * step, i * step, step, step, bounds, j == i) for j in range(i + 1)
            ]
            dq = jnp.zeros((step, 2 * HEAD_DIM), F32)
            for h in range(2):
                here = lane // HEAD_DIM == h
                q = jnp.where(here, q_ref[rows, :], 0)
                g = jnp.where(here, g_ref[rows, :], 0)
                delta = jnp.sum(products[h * HEAD_DIM : (h + 1) * HEAD_DIM], axis=0, keepdims=True)
                total = total_ref[0, h : h + 1, rows]
                for j in range(i + 1):
                    keys = slice(j * step, (j + 1) * step)
                    k = k_ref[keys, :]
                    scores = jnp.where(masks[j], dot(k, q, 1, 1) * SCORE_SCALE, -1e30)
                    p = jnp.exp2(scores - total)
                    back = (p * (dot(v_ref[keys, :], g, 1, 1) - delta)).astype(BF16)
                    dv = dot(p.astype(BF16), g)
                    dk = dot(back, q)
                    if j == i and h == 0:
                        dv_acc[keys, :] = dv
                        dk_acc[keys, :] = dk
                    else:
                        dv_acc[keys, :] += dv
                        dk_acc[keys, :] += dk
                    dq = dq + dot(back, jnp.where(here, k, 0), 0, 0)
            out_ref[rows, : 2 * HEAD_DIM] = (dq * HEAD_DIM**-0.5).astype(BF16)
        out_ref[:, 2 * HEAD_DIM : 4 * HEAD_DIM] = (dk_acc[...] * HEAD_DIM**-0.5).astype(BF16)
        out_ref[:, 4 * HEAD_DIM :] = dv_acc[...].astype(BF16)

    block = (group_rows, 2 * HEAD_DIM)
    return call(
        kernel,
        ends,
        [qkv, attended, attended_grad, totals],
        [
            ((group_rows, 6 * HEAD_DIM), lambda p, e: (0, first + p)),
            (block, lambda p, e: (0, first + p)),
            (block, lambda p, e: (0, first + p)),
            ((1, 2, group_rows), lambda p, e: (first + p, 0, 0)),
        ],
        [sds((group_rows, pairs * 6 * HEAD_DIM), BF16)],
        [((group_rows, 6 * HEAD_DIM), lambda p, e: (0, p))],
        (pairs,),
        scratch=[pltpu.VMEM(block, F32), pltpu.VMEM(block, F32)],
        flops=pairs * 10 * group_rows * group_rows * 2 * HEAD_DIM,
    )[0]


def project_out(core, mine, theirs, toks, pass_embed, weight, gain):
    rows, width = toks.shape
    tall, part = 256, width // 2

    def kernel(core_ref, mine_ref, theirs_ref, toks_ref, pass_ref, w_ref, gain_ref, mid_ref, normed_ref):
        def weight_rows(which):
            return w_ref[pl.ds(pl.multiple_of(which * part, part), part), :]

        mid = (
            toks_ref[...].astype(F32)
            + pass_ref[...]
            + dot(mine_ref[...], weight_rows(core_ref[0]))
            + dot(theirs_ref[...], weight_rows(1 - core_ref[0]))
        )
        mid_ref[...] = mid
        centred, scale = moments(mid)
        normed_ref[...] = (centred * scale * gain_ref[...]).astype(BF16)

    by_rows = ((tall, width), lambda i, c: (i, 0))
    half_rows = ((tall, part), lambda i, c: (i, 0))
    return call(
        kernel,
        core,
        [mine, theirs, toks, pass_embed, weight, gain],
        [half_rows, half_rows, by_rows, None, None, None],
        [sds((rows, width), F32), sds((rows, width), BF16)],
        [by_rows, by_rows],
        (rows // tall,),
        flops=2 * rows * width * width,
    )


def feed_forward(places, normed, cot_pairs, up_here, down_weight, block, chips, cuts):
    pieces = [p for pair in cot_pairs for p in pair[:2]]
    firsts = [pair[2] for pair in cot_pairs]
    width = normed.shape[1]
    rows, wide = normed.shape[0], 512
    half = rows // 2
    hidden = up_here.shape[1]
    per = hidden // chips
    here = wide // per
    view = down_weight.reshape(hidden // block, 2, block, width)
    n_cot = len(pieces)

    def kernel(at_ref, normed_ref, *refs):
        cot_refs = refs[:n_cot]
        up_ref, down_ref, active_ref, back_ref, cot_ref, *piles = refs[n_cot:]
        j = pl.program_id(0)

        def copy(ref, place):
            far, row = place
            start = jnp.where(far == 0, at_ref[0], 1 - at_ref[0]) * half + row
            cot_ref[pl.ds(pl.multiple_of(start, 16), ref.shape[0]), :] = ref[...]

        @pl.when(j == 0)
        def _():
            copy_picked(
                at_ref[1],
                [(cot_refs[2 * n], cot_refs[2 * n + 1], f) for n, f in enumerate(firsts)],
                copy,
            )

        upper = dot(normed_ref[...], up_ref[...])
        square = upper * upper
        bend = jnp.tanh(upper * (GELU_A + (GELU_A * GELU_B) * square))
        rise = 0.5 + 0.5 * bend
        active = (upper * rise).astype(BF16)
        active_ref[...] = active
        slope = 0.5 * GELU_A + (1.5 * GELU_A * GELU_B) * square
        steep = rise + upper * (slope * (1.0 - bend * bend))
        down = down_ref[...].reshape(wide, width)
        back_ref[...] = (dot(cot_ref[...], down, 1, 1) * steep).astype(BF16)
        grad = dot(active, cot_ref[...], 0, 0).astype(BF16)
        for r in range(here):
            row = r * per
            for n, cut in enumerate(cuts):
                piece = grad[row : row + cut]
                row += cut
                at = at_ref[2 + n * chips + j * here + r]
                gone_ref, kept_ref = piles[2 * n : 2 * n + 2]

                @pl.when(at < chips // 2)
                def _():
                    gone_ref[jnp.minimum(at, chips // 2 - 1)] = piece

                @pl.when(at >= chips // 2)
                def _():
                    kept_ref[jnp.maximum(at - chips // 2, 0)] = piece

    by_cols = ((rows, wide), lambda j, c: (0, j))
    piled = [sds((chips // 2, cut, width), BF16) for cut in cuts for _ in range(2)]
    active, back, cot, *piles = call(
        kernel,
        places,
        [normed, *pieces, up_here, view],
        [
            None,
            *[None] * n_cot,
            ((width, wide), lambda j, c: (0, j)),
            ((wide // block, None, block, width), lambda j, c: (j, c[2 + len(cuts) * chips], 0, 0)),
        ],
        [
            sds((rows, hidden), BF16),
            sds((rows, hidden), BF16),
            sds((rows, width), BF16),
            *piled,
        ],
        [by_cols, by_cols, None, *[None] * len(piled)],
        (hidden // wide,),
        flops=6 * rows * hidden * width,
    )
    return active, back, cot, [piles[2 * n : 2 * n + 2] for n in range(len(cuts))]


def rows_gradient(sources, tasks, chips, cores, heads):
    rows = tasks[0][0][0].shape[0]
    width = sum(piece.shape[1] for piece in tasks[0][0])
    single = len(tasks) == 1
    widths = [right.shape[1] for _, right in tasks]
    wide = 512 if single and widths[0] % 512 == 0 else max(widths)
    steps = widths[0] // wide if single else len(tasks)
    per = width // (chips * cores)
    inputs, in_blocks = [], []
    for lefts, right in tasks:
        inputs += [*lefts, right]
        in_blocks += [*[None] * len(lefts), ((rows, wide), lambda j, c: (0, j)) if single else None]

    def kernel(from_ref, *refs):
        gone_ref, kept_ref, turned_ref, tile_ref = refs[-4:]

        def turn(left_refs):
            column = 0
            for n, ref in enumerate(left_refs):
                size = ref.shape[1]
                to = column
                if len(left_refs) == 2:
                    to = pl.multiple_of(jnp.where(from_ref[chips] == n, 0, size), size)
                turned_ref[pl.ds(to, size), :] = jnp.transpose(ref[...])
                column += size

        def spread(columns, out_columns):
            for n in range(chips):
                number = from_ref[n]
                chip, head = number // heads, number % heads
                for k in range(cores):
                    start = pl.multiple_of(((chip * cores + k) * heads + head) * per, per)
                    ref = gone_ref if n < chips // 2 else kept_ref
                    ref[n % (chips // 2), k, :, out_columns] = tile_ref[pl.ds(start, per), columns]

        at, first = 0, 0
        for n, (lefts, right) in enumerate(tasks):
            left_refs, right_ref = refs[at : at + len(lefts)], refs[at + len(lefts)]
            at += len(lefts) + 1
            size = wide if single else widths[n]

            @pl.when(pl.program_id(0) == (0 if single else n))
            def _():
                turn(left_refs)

            @pl.when((pl.program_id(0) == n) | single)
            def _():
                tile_ref[:, :size] = dot(turned_ref[...], right_ref[...]).astype(BF16)
                spread(slice(0, size), slice(first, first + size))

            first += size

    total = sum(widths)
    block_columns = wide if single else total
    return call(
        kernel,
        sources,
        inputs,
        in_blocks,
        [sds((chips // 2, cores, per, total), BF16)] * 2,
        [
            ((chips // 2, cores, per, block_columns), lambda j, c: (0, 0, 0, j if single else 0))
        ]
        * 2,
        (steps,),
        scratch=[pltpu.VMEM((width, rows), BF16), pltpu.VMEM((width, wide), BF16)],
        flops=2 * rows * width * total,
    )


def rows_gradient_whole(core, left, right):
    rows, width = left.shape
    columns = right.shape[1]
    wide = 512 if columns % 512 == 0 else columns

    def kernel(core_ref, left_ref, right_ref, out_ref, turned_ref):
        @pl.when(pl.program_id(0) == 0)
        def _():
            turned_ref[...] = jnp.transpose(left_ref[...])

        out_ref[...] = dot(turned_ref[...], right_ref[...]).astype(BF16)

    return call(
        kernel,
        core,
        [left, right],
        [None, ((rows, wide), lambda j, c: (0, j))],
        [sds((width, columns), BF16)],
        [((width, wide), lambda j, c: (0, j))],
        (columns // wide,),
        scratch=[pltpu.VMEM((width, rows), BF16)],
        flops=2 * rows * width * columns,
    )[0]


def place_columns(core, pairs_of, shapes, moves):
    def kernel(core_ref, *refs):
        ins, outs = refs[: 2 * len(pairs_of)], refs[2 * len(pairs_of) :]
        c = core_ref[0]
        for pair, first, wide, out, column0, column1 in moves:
            for turn in range(2):
                k = c if turn == 0 else 1 - c
                to = pl.multiple_of(column0 + k * (column1 - column0), wide)
                outs[out][:, pl.ds(to, wide)] = ins[2 * pair + turn][:, first : first + wide]

    inputs = [a for pair in pairs_of for a in pair]
    return call(
        kernel,
        core,
        inputs,
        [None] * len(inputs),
        [sds(s, F32) for s in shapes],
        [None] * len(shapes),
        (1,),
    )


def back_through(core, back, weight):
    rows, hidden = back.shape
    width = weight.shape[0]
    wide = 512

    def kernel(core_ref, back_ref, w_ref, out_ref):
        out_ref[...] = dot(back_ref[...], w_ref[...], 1, 1).astype(BF16)

    return call(
        kernel,
        core,
        [back, weight],
        [None, ((wide, hidden), lambda n, c: (n, 0))],
        [sds((rows, width), BF16)],
        [((rows, wide), lambda n, c: (0, n))],
        (width // wide,),
        flops=2 * rows * hidden * width,
    )[0]


def project_down(core, active, weight, block):
    rows, hidden = active.shape
    width = weight.shape[1]
    half, wide = rows // 2, 512
    view = weight.reshape(hidden // block, 2, block, width)

    def kernel(core_ref, active_ref, w_ref, own_ref, gone_ref):
        def part(which):
            place = pl.ds(pl.multiple_of(which * half, half), half)
            return dot(active_ref[place, :], w_ref[...].reshape(hidden, wide))

        gone_ref[...] = part(1 - core_ref[0]).astype(BF16)
        own_ref[...] = part(core_ref[0])

    by_cols = ((half, wide), lambda n, c: (0, n))
    return call(
        kernel,
        core,
        [active, view],
        [None, ((hidden // block, None, block, wide), lambda n, c: (0, c[0], 0, n))],
        [sds((half, width), F32), sds((half, width), BF16)],
        [by_cols, by_cols],
        (width // wide,),
        flops=2 * rows * hidden * width,
    )


def back_to_attended(core, grad_mine, grad_theirs, mid, cot, gain, weight):
    rows, width = mid.shape
    tall, part = 256, width // 2

    def kernel(core_ref, gm_ref, gt_ref, mid_ref, cot_ref, gain_ref, w_ref, out_ref, cols_ref, mg_ref, gain_grad_ref):
        c = core_ref[0]
        incoming = gm_ref[...].astype(F32) + gt_ref[...].astype(F32)
        centred, scale = moments(mid_ref[...])
        x_hat = centred * scale
        terms = incoming * x_hat
        scaled = incoming * gain_ref[...]
        mean_a = jnp.mean(scaled, axis=-1, keepdims=True)
        mean_b = jnp.mean(terms * gain_ref[...], axis=-1, keepdims=True)
        mid_grad = cot_ref[...].astype(F32) + scale * (scaled - mean_a - x_hat * mean_b)
        mg_ref[...] = mid_grad
        branch = mid_grad.astype(BF16)
        out_ref[...] = dot(branch, w_ref[pl.ds(pl.multiple_of(c * part, part), part), :], 1, 1).astype(BF16)
        cols_ref[...] = jnp.where(c == 0, branch[:, :part], branch[:, part:])

        @pl.when(pl.program_id(0) == 0)
        def _():
            gain_grad_ref[...] = jnp.zeros_like(gain_grad_ref)

        gain_grad_ref[...] += jnp.sum(terms.reshape(tall // 8, 8, width), axis=0)

    by_rows = ((tall, width), lambda i, c: (i, 0))
    half_rows = ((tall, part), lambda i, c: (i, 0))
    return call(
        kernel,
        core,
        [grad_mine, grad_theirs, mid, cot, gain, weight],
        [by_rows, by_rows, by_rows, by_rows, None, None],
        [
            sds((rows, part), BF16),
            sds((rows, part), BF16),
            sds((rows, width), F32),
            sds((8, width), F32),
        ],
        [half_rows, half_rows, by_rows, None],
        (rows // tall,),
        flops=rows * width * width,
    )


def back_through_qkv(core, backs, weight):
    rows = backs[0].shape[0]
    width, columns = weight.shape
    half, wide = rows // 2, 512

    def kernel(core_ref, *refs):
        back_refs, (w_ref, own_ref, gone_ref) = refs[: len(backs)], refs[len(backs) :]

        def some(which):
            place = pl.ds(pl.multiple_of(which * half, half), half)
            total, first = 0.0, 0
            for ref in back_refs:
                last = first + ref.shape[1]
                total = total + dot(ref[place, :], w_ref[:, first:last], 1, 1)
                first = last
            return total

        gone_ref[...] = some(1 - core_ref[0]).astype(BF16)
        own_ref[...] = some(core_ref[0])

    by_cols = ((half, wide), lambda n, c: (0, n))
    return call(
        kernel,
        core,
        [*backs, weight],
        [*[None] * len(backs), ((wide, columns), lambda n, c: (n, 0))],
        [sds((half, width), F32), sds((half, width), BF16)],
        [by_cols, by_cols],
        (width // wide,),
        flops=2 * rows * columns * width,
    )


def back_to_tokens(core, grad_own, grad_came, toks, pass_embed, gain, mid_grad):
    half, width = grad_own.shape
    tall = 256
    steps = half // tall

    def kernel(core_ref, own_ref, came_ref, toks_ref, pass_ref, gain_ref, mg_ref, out_ref, sums_ref):
        incoming = own_ref[...] + came_ref[...].astype(F32)
        centred, scale = moments(toks_ref[...].astype(F32) + pass_ref[...])
        x_hat = centred * scale
        terms = incoming * x_hat
        scaled = incoming * gain_ref[...]
        mean_a = jnp.mean(scaled, axis=-1, keepdims=True)
        mean_b = jnp.mean(terms * gain_ref[...], axis=-1, keepdims=True)
        resid_grad = mg_ref[...] + scale * (scaled - mean_a - x_hat * mean_b)
        out_ref[...] = resid_grad.astype(BF16)

        @pl.when(pl.program_id(0) == 0)
        def _():
            sums_ref[...] = jnp.zeros_like(sums_ref)

        sums_ref[0] += jnp.sum(resid_grad.reshape(tall // 8, 8, width), axis=0)
        sums_ref[1] += jnp.sum(terms.reshape(tall // 8, 8, width), axis=0)

    by_rows = ((tall, width), lambda i, c: (i, 0))
    own_rows = ((tall, width), lambda i, c: (c[0] * steps + i, 0))
    return call(
        kernel,
        core,
        [grad_own, grad_came, toks, pass_embed, gain, mid_grad],
        [by_rows, by_rows, own_rows, None, None, own_rows],
        [sds((half, width), BF16), sds((2, 8, width), F32)],
        [by_rows, None],
        (steps,),
        flops=20 * half * width,
    )


def body(
    sizes,
    tokens,
    seq_lengths,
    pass_embed,
    norm1_gain,
    qkv_weight,
    out_weight,
    norm2_gain,
    up_weight,
    down_weight,
    cotangent,
):
    n_chip, n_core, n_half, n_lane = sizes
    n_head = n_half * n_lane
    tok_rows, width = tokens.shape
    rows = 2 * tok_rows
    group_rows = tok_rows * n_head
    hidden = up_weight.shape[1]
    core = lax.axis_index("core")
    chip = lax.axis_index("chip")
    half = lax.axis_index("half")
    head = half * n_lane + lax.axis_index("lane")
    line = {"turn": [], "riders": []}
    core_row = jnp.reshape(core, (1,)).astype(jnp.int32)
    core_at = (core_row, line)
    pass_row, gain1, gain2 = (v.reshape(1, width) for v in (pass_embed, norm1_gain, norm2_gain))

    def index(c, k, h, l):
        return ((c * n_core + k) * n_half + h) * n_lane + l

    everyone = [
        (c, k, h, l)
        for c in range(n_chip)
        for k in range(n_core)
        for h in range(n_half)
        for l in range(n_lane)
    ]
    def across_chip(pick):
        return [
            (index(c, k, h, l), index(c, 1 - k, h, l)) for c, k, h, l in everyone if pick(k, h)
        ]

    def stay(k, h):
        return k == h

    def leave(k, h):
        return k != h

    leavers = [d for d in everyone if leave(d[1], d[2])]
    regroup_perm = [(index(c, k, h, l), index(c, h, k, l)) for c, k, h, l in leavers]
    beside_perm = [(index(c, k, h, l), index(c, k, 1 - h, l)) for c, k, h, l in leavers]

    def send(value, pairs):
        return lax.ppermute(value, AXES, pairs)

    def regroup(value):
        return jnp.where(core == half, value, send(value, regroup_perm))

    def across(value):
        return lax.ppermute(value, "core", [(0, 1), (1, 0)])

    n_chips = n_chip * n_head
    n_bits = n_chips.bit_length() - 1
    number = chip * n_head + head
    bits = list(range(n_bits))
    near = ([0, 1, *bits[2:]], [1, 0, *bits[2:]])
    far_first = ([*bits[2:], 0, 1], [*bits[2:], 1, 0])

    def of_core(pair):
        return jnp.where(core == 0, jnp.asarray(pair[0], jnp.int32), jnp.asarray(pair[1], jnp.int32))

    def spread(order):
        return [
            sum(((p >> (n_bits - 1 - s)) & 1) << order[s] for s in range(1, n_bits))
            for p in range(n_chips // 2)
        ]

    def bit(orders, step):
        return (number >> of_core([o[step] for o in orders])) & 1

    def sources(orders):
        rest = of_core([spread(o) for o in orders])
        first = of_core([o[0] for o in orders])
        mine = bit(orders, 0)
        return jnp.concatenate([rest + ((1 - mine) << first), rest + (mine << first)])

    def places(orders):
        inside = []
        for o in orders:
            found = spread(o)
            inside.append([found.index(n & ~(1 << o[0])) for n in range(n_chips)])
        first = of_core([[(n >> o[0]) & 1 for n in range(n_chips)] for o in orders])
        kept = first == bit(orders, 0)
        return of_core(inside) + jnp.where(kept, n_chips // 2, 0)

    def flip(orders, step):
        def partner(c, k, h, l):
            other = (c * n_head + h * n_lane + l) ^ (1 << orders[k][step])
            return index(other // n_head, k, other % n_head // n_lane, other % n_lane)

        return [(index(*d), partner(*d)) for d in everyone]

    def sum_over_chips(orders, gone, kept):
        parts, ats = [kept], []

        def send_blocks(blocks):
            parts.append(lax.ppermute(blocks, AXES, flip(orders, len(parts) - 1)))

        def starts(last):
            found = []
            for k in range(len(parts)):
                value = 0
                for b in [*ats[max(k - 1, 0) :], *last]:
                    value = value * 2 + b
                found.append(jnp.asarray(value, jnp.int32))
            return found

        def next_step():
            step = len(parts) - 1
            at = bit(orders, step)
            found = starts([1 - at])
            ats.append(at)
            return jnp.stack(found), list(parts), n_chips >> (step + 1)

        def total(which, count):
            return sum(
                lax.dynamic_slice_in_dim(p, s * count, count, 0).astype(F32)
                for p, s in zip(parts, which)
            )

        def ride():
            line["riders"].append({"next_step": next_step, "send": send_blocks})

        def advance():
            found, _, count = next_step()
            send_blocks(total(found, count).astype(BF16))

        def finish():
            while len(parts) - 1 < n_bits:
                advance()
            if kept.ndim == 3:
                return total(starts([]), 1)[0]
            pair = []
            for k in (core, 1 - core):
                rows_k = [lax.dynamic_index_in_dim(p, k, 1, keepdims=False) for p in parts]
                pair.append(
                    sum(
                        lax.dynamic_index_in_dim(p, s, 0, keepdims=False).astype(F32)
                        for p, s in zip(rows_k, starts([]))
                    )
                )
            return pair[0], across(pair[1])

        send_blocks(gone)
        return {"ride": ride, "advance": advance, "finish": finish}

    def split(whole, orders):
        view = whole.reshape((2,) * n_bits + whole.shape[1:])
        tail = tuple(range(n_bits, view.ndim))
        turned = [
            jnp.transpose(view, tuple(n_bits - 1 - b for b in o) + tail) for o in orders
        ]
        at = bit(orders, 0)

        def take(where):
            found = [lax.dynamic_index_in_dim(t, where, 0, keepdims=False) for t in turned]
            return jnp.where(core == 0, *found).reshape((n_chips // 2,) + whole.shape[1:])

        return take(1 - at), take(at)

    per = width // (n_chips * n_core)

    def gradient(orders, *tasks):
        if per % 16 == 0:
            chosen = jnp.concatenate([sources(orders), core_row])
            return rows_gradient((chosen, line), tasks, n_chips, n_core, n_head)
        wholes = []
        for lefts, right in tasks:
            left = lefts[0]
            if len(lefts) == 2:
                left = jnp.where(
                    core == 0, jnp.concatenate(lefts, axis=1), jnp.concatenate(lefts[::-1], axis=1)
                )
            wholes.append(rows_gradient_whole(core_at, left, right))
        whole = jnp.concatenate(wholes, axis=1)
        view = whole.reshape(n_chip, n_core, n_head, per, whole.shape[1])
        return split(jnp.swapaxes(view, 1, 2).reshape(n_chips, n_core, per, -1), orders)

    part = width // 2
    ff_block = hidden // (n_chip * n_core)
    core_pairs = part // (2 * HEAD_DIM)
    stays = (core == half).astype(jnp.int32)
    cut = tok_rows // 2

    def spread_group(value):
        near_came = send(value, across_chip(stay))
        top_came = send(value[:cut], regroup_perm)
        low_came = send(value[cut:], beside_perm)
        return near_came, top_came, low_came

    def pass_on(value, came, done):
        near_came, top_came, low_came = came
        later = (done[:1, :1] * 0).astype(BF16)
        top_came, low_came = top_came + later, low_came + later
        top_on = send(top_came, across_chip(leave))
        low_on = send(low_came, across_chip(stay))
        near = [(value, near_came, (0, 0))]
        far = [(top_on, top_came, (1, 0)), (low_came, low_on, (1, cut))]
        return near, far

    tokens_came = spread_group(tokens)
    lengths_came = send(seq_lengths, across_chip(stay))
    up_here, qkv_here = weights_here(core_at, up_weight, qkv_weight, ff_block)
    near_toks = [(tokens, tokens_came[0], (0, 0))]
    first_half = project_qkv(
        (jnp.stack([half, stays]), line), [p[:2] for p in near_toks], pass_row, gain1, qkv_here
    )
    _, far_toks = pass_on(tokens, tokens_came, up_here)
    toks, normed_a, qkv = project_qkv(
        (jnp.stack([1 - half, stays]), line),
        [p[:2] for p in far_toks],
        pass_row,
        gain1,
        qkv_here,
        first_half,
    )
    cotangent, tokens_done = lax.optimization_barrier((cotangent, tokens_came))
    cot_came = spread_group(cotangent)
    lengths = jnp.where(core == half, seq_lengths, lengths_came)[0]
    order = jnp.arange(lengths.shape[0])
    ends = jnp.sum(jnp.where(order[:, None] <= order[None, :], lengths[:, None], 0), axis=0)

    def to_heads(value):
        value = lax.all_to_all(value, "lane", split_axis=1, concat_axis=0, tiled=True)
        value = value.reshape(n_lane, 2, tok_rows, -1)
        return jnp.swapaxes(value, 0, 1).reshape(group_rows, -1)

    def from_heads(value):
        value = value.reshape(2, n_lane, tok_rows, -1)
        value = jnp.swapaxes(value, 0, 1).reshape(group_rows, -1)
        return lax.all_to_all(value, "lane", split_axis=0, concat_axis=1, tiled=True)

    if n_lane > 1:
        qkv = to_heads(qkv)
    pairs = core_pairs // n_lane
    near_cot, far_cot = pass_on(cotangent, cot_came, toks)
    attended_heads, totals = attend((ends, line), qkv)
    mine = from_heads(attended_heads) if n_lane > 1 else attended_heads
    theirs = across(mine)

    middle, normed_m = project_out(
        core_at, mine, theirs, toks, pass_row, out_weight, gain2
    )
    per_ff = hidden // 2 // n_chips
    down_orders, cuts = [near], [per_ff]
    if per_ff % 32 == 0 and n_bits > 3:
        down_orders, cuts = [far_first, near], [per_ff // 2] * 2
    active, upper_grad, cot, piles = feed_forward(
        (
            jnp.concatenate(
                [jnp.stack([half, stays]), *[places(o) for o in down_orders], core_row]
            ),
            line,
        ),
        normed_m,
        [*near_cot, *far_cot],
        up_here,
        down_weight,
        ff_block,
        n_chips,
        cuts,
    )
    down_sums = [sum_over_chips(o, *pile) for o, pile in zip(down_orders, piles)]
    normed_m_part = back_through(core_at, upper_grad, up_here)
    normed_m_came = across(normed_m_part)
    up_sum = sum_over_chips(near, *gradient(near, ([normed_m], upper_grad)))
    if len(down_sums) > 1:
        down_sums[1]["ride"]()
    attended_grad, branch_cols, middle_grad, norm2_terms = back_to_attended(
        core_at, normed_m_part, normed_m_came, middle, cot, gain2, out_weight
    )
    if n_lane > 1:
        attended_grad = to_heads(attended_grad)

    half_pairs = pairs if n_lane > 1 else max(1, pairs // 2)

    def back_pairs(first):
        back = attend_back(
            (ends, line), qkv, attended_heads, attended_grad, totals, first, half_pairs
        )
        return from_heads(back) if n_lane > 1 else back

    down_sums[0]["ride"]()
    backs = [back_pairs(0)]
    rest_sums = [
        sum_over_chips(
            near,
            *gradient(near, ([normed_a], backs[0]), ([mine, theirs], branch_cols)),
        )
    ]
    if half_pairs < pairs:
        up_sum["ride"]()
        backs.append(back_pairs(half_pairs))
        for s in down_sums:
            s["ride"]()
        rest_sums.append(sum_over_chips(near, *gradient(near, ([normed_a], backs[1]))))
    normed_a_own, normed_a_gone = back_through_qkv(core_at, backs, qkv_here)
    normed_a_came = across(normed_a_gone)
    rest_sums[0]["ride"]()
    output_own, output_gone = project_down(core_at, active, down_weight, ff_block)
    output_came = across(output_gone)
    for s in down_sums:
        s["ride"]()
    token_grad, sums = back_to_tokens(
        core_at, normed_a_own, normed_a_came, toks, pass_row, gain1, middle_grad
    )
    token_grad = regroup(token_grad)
    middle_own = lax.dynamic_slice_in_dim(middle, core * tok_rows, tok_rows, 0)
    mixed = regroup((middle_own + output_own + output_came.astype(F32)).astype(BF16))

    down_grad = jnp.concatenate([s["finish"]() for s in down_sums], axis=0)
    up_pair = up_sum["finish"]()
    (up_grad,) = place_columns(
        core_at,
        [up_pair],
        [(per, hidden)],
        [
            (0, n * ff_block, ff_block, 0, 2 * n * ff_block, (2 * n + 1) * ff_block)
            for n in range(n_chip)
        ],
    )
    pairs_of = [s["finish"]() for s in rest_sums]
    size = 3 * part // len(rest_sums)
    moves = [(0, size, part, 0, 0, part)]
    two = 2 * HEAD_DIM
    for n in range(3):
        for lane in range(n_lane):
            for r in range(len(rest_sums)):
                for p in range(half_pairs):
                    first = ((lane * half_pairs + p) * 3 + n) * two
                    column = n * width + (lane * pairs + r * half_pairs + p) * two
                    moves.append((r, first, two, 1, column, column + part))
    out_grad, qkv_grad = place_columns(
        core_at, pairs_of, [(per, width), (per, 3 * width)], moves
    )

    small = jnp.sum(jnp.concatenate([sums, 0.5 * norm2_terms[None]]), axis=1)
    n_all = len(everyone)
    small = jnp.swapaxes(small.reshape(3, n_all, width // n_all), 0, 1)
    small = lax.all_to_all(small, AXES, split_axis=0, concat_axis=0, tiled=True)
    small = jnp.sum(small, axis=0)
    return (
        mixed,
        token_grad,
        small[0],
        small[1],
        qkv_grad,
        out_grad,
        small[2],
        up_grad,
        down_grad,
    )


def solution(mesh):
    n_dp, n_head = mesh.shape["dp"], mesh.shape["head"]
    sizes = (n_dp // 2, 2, 2, n_head // 2)
    fine = Mesh(mesh.devices.reshape(sizes), AXES)
    rows, group = P(AXES), P(("chip", "core"))
    in_specs = (rows, group, P(), P(), P(), P(), P(), P(), P(), rows)
    return jax.shard_map(
        partial(body, sizes),
        mesh=fine,
        in_specs=in_specs,
        out_specs=(rows,) * 9,
        check_vma=False,
    )
```

```python
from functools import partial

import jax
import jax.numpy as jnp
from jax import lax
from jax.experimental import pallas as pl
from jax.experimental.pallas import tpu as pltpu
from jax.sharding import Mesh, PartitionSpec as P

HEADS = 16
HEAD_DIM = 64
AXES = ("chip", "core", "half", "lane")
F32 = jnp.float32
BF16 = jnp.bfloat16
COST = 20
COSTS = {9: 0.001, 8: 200, 2: 0.1, 17: 0.1, 0: 0.001, 1: 0.1, 18: 200, 7: 5, 5: 5, 14: 200, 15: 200, 6: 20}
RIDES = {10: 'ba', 12: 'b', 13: 'u', 14: 'bar', 15: 'au', 16: 'rs', 17: 's', 18: 'u', 20: 'rs'}
SCORE_SCALE = HEAD_DIM**-0.5 * 1.4426950408889634
GELU_A, GELU_B = 0.7978845608028654, 0.044715


def call(kernel, line, inputs, in_blocks, out_shapes, out_blocks, grid, scratch=(), flops=0, aliases=None, more=()):
    (steps,) = grid
    n_in, n_out, body = len(inputs), len(out_shapes), kernel
    waits = [*line["turn"], *line["after"]]
    inputs, in_blocks = [*inputs, *waits], [*in_blocks, *["any"] * len(waits)]
    out_shapes, out_blocks = [*out_shapes, sds((8, 128), F32)], [*out_blocks, "any"]
    riders, works = [line["sums"][name] for name in line["rides"].get(line["count"], ())], []
    line["after"] = []
    for rider in riders:
        parts, wanted = rider["next_step"]()
        tail = parts[0].shape[1:]
        zeros = (0,) * len(tail)
        for starts, count in wanted:
            per = count // steps if count % steps == 0 else 1
            blocks = count // per
            works.append((rider, len(inputs), len(parts), len(out_shapes)))
            for part, at in zip(parts, starts, strict=True):
                inputs.append(part)
                in_blocks.append(
                    (
                        (per, *tail),
                        lambda g, s, at=at, b=blocks, z=zeros: (s[at] * b + jnp.minimum(g, b - 1), *z),
                    )
                )
            out_shapes.append(sds((count, *tail), BF16))
            out_blocks.append(
                ((per, *tail), lambda g, s, b=blocks, z=zeros: (jnp.minimum(g, b - 1), *z))
            )

    def kernel(*refs):
        numbers, refs = refs[: 1 + len(more)], refs[1 + len(more) :]
        ins, outs = refs[: len(inputs)], refs[len(inputs) : len(inputs) + len(out_shapes)]
        rest = refs[len(inputs) + len(out_shapes) :]
        body(*numbers, *ins[:n_in], *outs[:n_out], *rest)
        for _, first, width, out in works:
            outs[out][...] = sum(r[...].astype(F32) for r in ins[first : first + width]).astype(BF16)

    def spec(array, block):
        if block is None:
            rank = len(array.shape)
            return pl.BlockSpec(array.shape, lambda *_: (0,) * rank)
        if block == "any":
            return pl.BlockSpec(memory_space=pl.ANY)
        return pl.BlockSpec(block[0], lambda g, s, *_: block[1](g, s))

    moved = sum(a.size * a.dtype.itemsize for a in (*inputs, *out_shapes))
    weight = line["cost"].get(line["count"], COST)
    line["count"] += 1
    outs = pl.pallas_call(
        kernel,
        out_shape=out_shapes,
        grid_spec=pltpu.PrefetchScalarGridSpec(
            num_scalar_prefetch=1 + len(more),
            grid=grid,
            in_specs=[spec(a, b) for a, b in zip(inputs, in_blocks, strict=True)],
            out_specs=[spec(a, b) for a, b in zip(out_shapes, out_blocks, strict=True)],
            scratch_shapes=list(scratch),
        ),
        compiler_params=pltpu.CompilerParams(vmem_limit_bytes=56 * 2**20),
        cost_estimate=pl.CostEstimate(
            flops=int(flops * weight), bytes_accessed=int(moved * weight), transcendentals=0
        ),
        input_output_aliases={k + len(more): v for k, v in (aliases or {}).items()},
    )(line["here"], *more, *inputs)
    line["turn"] = [outs[n_out]]
    for rider in riders:
        rider["send"]([outs[out] for who, _, _, out in works if who is rider])
    return list(outs[:n_out])


def sds(shape, dtype):
    return jax.ShapeDtypeStruct(shape, dtype)


def moments(hidden):
    row_mean = jnp.mean(hidden, axis=-1, keepdims=True)
    centred = hidden - row_mean
    variance = jnp.mean(centred * centred, axis=-1, keepdims=True)
    return centred, lax.rsqrt(variance + 1e-05)


def dot(a, b, ca=1, cb=0):
    return lax.dot_general(a, b, (((ca,), (cb,)), ((), ())), preferred_element_type=F32)


CORE, HALF, STAYS, OTHER_HALF, TABLES = range(5)


def qkv_columns(line, weight):
    width = weight.shape[0]
    tall, two = 256, 2 * HEAD_DIM
    pairs = width // 2 // two

    def kernel(here, in_ref, out_ref):
        for p in range(pairs):
            for t in range(3):
                start = pl.multiple_of(t * width + here[CORE] * (width // 2) + p * two, two)
                to = (3 * p + t) * two
                out_ref[:, to : to + two] = in_ref[:, pl.ds(start, two)]

    return copy_rows(line, kernel, weight, tall)


def up_columns(line, weight, block):
    hidden = weight.shape[1]

    def kernel(here, in_ref, out_ref):
        for n in range(hidden // 2 // block):
            start = pl.multiple_of((2 * n + here[CORE]) * block, block)
            out_ref[:, n * block : (n + 1) * block] = in_ref[:, pl.ds(start, block)]

    return copy_rows(line, kernel, weight, 256)


def copy_rows(line, kernel, weight, tall):
    rows, columns = weight.shape

    def by_rows(wide):
        return ((tall, wide), lambda i, c: (i, 0))

    return call(
        kernel,
        line,
        [weight],
        [by_rows(columns)],
        [sds((rows, columns // 2), BF16)],
        [by_rows(columns // 2)],
        (rows // tall,),
    )[0]


def copy_picked(stays, pairs, copy):
    for here, came, row in pairs:
        @pl.when(stays == 1)
        def _():
            copy(here, row)

        @pl.when(stays != 1)
        def _():
            copy(came, row)


def project_qkv(line, at, pairs, pass_embed, gain, weight, into=None):
    pieces = [p for pair in pairs for p in pair]
    width = pieces[0].shape[1]
    heights = [pair[0].shape[0] for pair in pairs]
    half = sum(heights)
    rows, wide = 2 * half, 512
    columns = weight.shape[1]

    def kernel(here, *refs):
        piece_refs, (pass_ref, gain_ref, w_ref, *refs) = refs[: len(pieces)], refs[len(pieces) :]
        toks_ref, normed_ref, qkv_ref = refs[-3:]

        def norm_rows(ref, row):
            for start in range(0, ref.shape[0], 64):
                low = ref[start : start + 64, :]
                centred, scale = moments(low.astype(F32) + pass_ref[...])
                to = slice(row + start, row + start + 64)
                toks_ref[to, :] = low
                normed_ref[to, :] = (centred * scale * gain_ref[...]).astype(BF16)

        @pl.when(pl.program_id(0) == 0)
        def _():
            firsts = [sum(heights[:n]) for n in range(len(pairs))]
            copy_picked(
                here[STAYS],
                [(piece_refs[2 * n], piece_refs[2 * n + 1], f) for n, f in enumerate(firsts)],
                norm_rows,
            )

        qkv_ref[...] = dot(normed_ref[...], w_ref[...]).astype(BF16)

    inputs = [*pieces, pass_embed, gain, weight]
    in_blocks = [*[None] * (len(pieces) + 2), ((width, wide), lambda j, a: (0, j))]
    aliases = {}
    if into is not None:
        aliases = {len(inputs) + 1 + n: n for n in range(3)}
        inputs += into
        in_blocks += ["any"] * 3
    all_rows = ((half, width), lambda j, a: (a[at], 0))
    return call(
        kernel,
        line,
        inputs,
        in_blocks,
        [sds((rows, width), BF16), sds((rows, width), BF16), sds((rows, columns), BF16)],
        [all_rows, all_rows, ((half, wide), lambda j, a: (a[at], j))],
        (columns // wide,),
        flops=rows * width * columns,
        aliases=aliases,
    )


def allowed(first_key, first_query, keys, queries, ends, diagonal):
    at_query = first_query + lax.broadcasted_iota(jnp.int32, (1, queries), 1)
    start = jnp.zeros_like(at_query)
    for end in ends:
        start = jnp.where(at_query >= end, end, start)
    at_key = first_key + lax.broadcasted_iota(jnp.int32, (keys, queries), 0)
    mask = at_key >= start
    if diagonal:
        mask = mask & (at_key <= at_query)
    return mask


def attention_block(group_rows):
    return 256 if group_rows <= 1024 else 512


def attend(line, ends, qkv):
    group_rows, columns = qkv.shape
    pairs = columns // (6 * HEAD_DIM)
    step = attention_block(group_rows)
    n_ends = ends.shape[0]

    def kernel(here, ends_ref, qkv_ref, o_ref, total_ref, vt_ref):
        q_ref, k_ref, v_ref = (qkv_ref.at[:, pl.ds(2 * HEAD_DIM * n, 2 * HEAD_DIM)] for n in range(3))
        bounds = [ends_ref[n] for n in range(n_ends)]
        vt_ref[...] = jnp.transpose(v_ref[...])
        lane = lax.broadcasted_iota(jnp.int32, (1, 2 * HEAD_DIM), 1)
        for i in range(group_rows // step):
            rows = slice(i * step, (i + 1) * step)
            outs = []
            masks = [
                allowed(j * step, i * step, step, step, bounds, j == i) for j in range(i + 1)
            ]
            for h in range(2):
                q = jnp.where(lane // HEAD_DIM == h, q_ref[rows, :], 0)
                scores = [
                    jnp.where(
                        masks[j],
                        dot(k_ref[j * step : (j + 1) * step, :], q, 1, 1) * SCORE_SCALE,
                        -1e30,
                    )
                    for j in range(i + 1)
                ]
                top = jnp.max(scores[0], axis=0, keepdims=True)
                for s in scores[1:]:
                    top = jnp.maximum(top, jnp.max(s, axis=0, keepdims=True))
                total = jnp.zeros_like(top)
                out = jnp.zeros((HEAD_DIM, step), F32)
                for j in range(i + 1):
                    p = jnp.exp2(scores[j] - top)
                    total = total + jnp.sum(p, axis=0, keepdims=True)
                    out = out + dot(
                        vt_ref[h * HEAD_DIM : (h + 1) * HEAD_DIM, j * step : (j + 1) * step],
                        p.astype(BF16),
                    )
                outs.append(out * (1.0 / total))
                total_ref[0, h : h + 1, rows] = top + jnp.log2(total)
            o_ref[rows, :] = jnp.transpose(jnp.concatenate(outs, axis=0)).astype(BF16)

    block = (group_rows, 2 * HEAD_DIM)
    return call(
        kernel,
        line,
        [qkv],
        [((group_rows, 6 * HEAD_DIM), lambda p, e: (0, p))],
        [
            sds((group_rows, pairs * 2 * HEAD_DIM), BF16),
            sds((pairs, 2, group_rows), F32),
        ],
        [(block, lambda p, e: (0, p)), ((1, 2, group_rows), lambda p, e: (p, 0, 0))],
        (pairs,),
        scratch=[pltpu.VMEM((2 * HEAD_DIM, group_rows), BF16)],
        flops=pairs * 4 * group_rows * group_rows * 2 * HEAD_DIM,
        more=[ends],
    )


def attend_back(line, ends, qkv, attended, attended_grad, totals, first, pairs):
    group_rows = qkv.shape[0]
    step = attention_block(group_rows)
    n_ends = ends.shape[0]

    def kernel(here, ends_ref, qkv_ref, o_ref, g_ref, total_ref, out_ref, dk_acc, dv_acc):
        q_ref, k_ref, v_ref = (qkv_ref.at[:, pl.ds(2 * HEAD_DIM * n, 2 * HEAD_DIM)] for n in range(3))
        bounds = [ends_ref[n] for n in range(n_ends)]
        lane = lax.broadcasted_iota(jnp.int32, (1, 2 * HEAD_DIM), 1)
        for i in range(group_rows // step):
            rows = slice(i * step, (i + 1) * step)
            products = jnp.transpose(g_ref[rows, :].astype(F32) * o_ref[rows, :].astype(F32))
            masks = [
                allowed(j * step, i * step, step, step, bounds, j == i) for j in range(i + 1)
            ]
            dq = jnp.zeros((step, 2 * HEAD_DIM), F32)
            for h in range(2):
                here = lane // HEAD_DIM == h
                q = jnp.where(here, q_ref[rows, :], 0)
                g = jnp.where(here, g_ref[rows, :], 0)
                delta = jnp.sum(products[h * HEAD_DIM : (h + 1) * HEAD_DIM], axis=0, keepdims=True)
                total = total_ref[0, h : h + 1, rows]
                for j in range(i + 1):
                    keys = slice(j * step, (j + 1) * step)
                    k = k_ref[keys, :]
                    scores = jnp.where(masks[j], dot(k, q, 1, 1) * SCORE_SCALE, -1e30)
                    p = jnp.exp2(scores - total)
                    back = (p * (dot(v_ref[keys, :], g, 1, 1) - delta)).astype(BF16)
                    dv = dot(p.astype(BF16), g)
                    dk = dot(back, q)
                    if j == i and h == 0:
                        dv_acc[keys, :] = dv
                        dk_acc[keys, :] = dk
                    else:
                        dv_acc[keys, :] += dv
                        dk_acc[keys, :] += dk
                    dq = dq + dot(back, jnp.where(here, k, 0), 0, 0)
            out_ref[rows, : 2 * HEAD_DIM] = (dq * HEAD_DIM**-0.5).astype(BF16)
        out_ref[:, 2 * HEAD_DIM : 4 * HEAD_DIM] = (dk_acc[...] * HEAD_DIM**-0.5).astype(BF16)
        out_ref[:, 4 * HEAD_DIM :] = dv_acc[...].astype(BF16)

    block = (group_rows, 2 * HEAD_DIM)
    return call(
        kernel,
        line,
        [qkv, attended, attended_grad, totals],
        [
            ((group_rows, 6 * HEAD_DIM), lambda p, e: (0, first + p)),
            (block, lambda p, e: (0, first + p)),
            (block, lambda p, e: (0, first + p)),
            ((1, 2, group_rows), lambda p, e: (first + p, 0, 0)),
        ],
        [sds((group_rows, pairs * 6 * HEAD_DIM), BF16)],
        [((group_rows, 6 * HEAD_DIM), lambda p, e: (0, p))],
        (pairs,),
        scratch=[pltpu.VMEM(block, F32), pltpu.VMEM(block, F32)],
        flops=pairs * 10 * group_rows * group_rows * 2 * HEAD_DIM,
        more=[ends],
    )[0]


def project_out(line, mine, theirs, toks, pass_embed, weight, gain):
    rows, width = toks.shape
    tall, part = 256, width // 2

    def kernel(here, mine_ref, theirs_ref, toks_ref, pass_ref, w_ref, gain_ref, mid_ref, normed_ref):
        def weight_rows(which):
            return w_ref[pl.ds(pl.multiple_of(which * part, part), part), :]

        mid = (
            toks_ref[...].astype(F32)
            + pass_ref[...]
            + dot(mine_ref[...], weight_rows(here[CORE]))
            + dot(theirs_ref[...], weight_rows(1 - here[CORE]))
        )
        mid_ref[...] = mid
        centred, scale = moments(mid)
        normed_ref[...] = (centred * scale * gain_ref[...]).astype(BF16)

    by_rows = ((tall, width), lambda i, c: (i, 0))
    half_rows = ((tall, part), lambda i, c: (i, 0))
    return call(
        kernel,
        line,
        [mine, theirs, toks, pass_embed, weight, gain],
        [half_rows, half_rows, by_rows, None, None, None],
        [sds((rows, width), F32), sds((rows, width), BF16)],
        [by_rows, by_rows],
        (rows // tall,),
        flops=2 * rows * width * width,
    )


def feed_forward(line, places, normed, cot_pairs, up_here, down_weight, block, chips, cuts):
    pieces = [p for pair in cot_pairs for p in pair[:2]]
    firsts = [pair[2] for pair in cot_pairs]
    width = normed.shape[1]
    rows, wide = normed.shape[0], 512
    half = rows // 2
    hidden = up_here.shape[1]
    per = hidden // chips
    many = wide // per
    view = down_weight.reshape(hidden // block, 2, block, width)
    n_cot = len(pieces)

    def kernel(here, normed_ref, *refs):
        cot_refs = refs[:n_cot]
        up_ref, down_ref, active_ref, back_ref, cot_ref, *piles = refs[n_cot:]
        j = pl.program_id(0)

        def copy(ref, place):
            far, row = place
            start = here[HALF if far == 0 else OTHER_HALF] * half + row
            cot_ref[pl.ds(pl.multiple_of(start, 16), ref.shape[0]), :] = ref[...]

        @pl.when(j == 0)
        def _():
            copy_picked(
                here[STAYS],
                [(cot_refs[2 * n], cot_refs[2 * n + 1], f) for n, f in enumerate(firsts)],
                copy,
            )

        upper = dot(normed_ref[...], up_ref[...])
        square = upper * upper
        bend = jnp.tanh(upper * (GELU_A + (GELU_A * GELU_B) * square))
        rise = 0.5 + 0.5 * bend
        active = (upper * rise).astype(BF16)
        active_ref[...] = active
        slope = 0.5 * GELU_A + (1.5 * GELU_A * GELU_B) * square
        steep = rise + upper * (slope * (1.0 - bend * bend))
        down = down_ref[...].reshape(wide, width)
        back_ref[...] = (dot(cot_ref[...], down, 1, 1) * steep).astype(BF16)
        grad = dot(active, cot_ref[...], 0, 0).astype(BF16)
        for r in range(many):
            row = r * per
            for n, cut in enumerate(cuts):
                piece = grad[row : row + cut]
                row += cut
                at = here[places[n] + j * many + r]
                gone_ref, kept_ref = piles[2 * n : 2 * n + 2]

                @pl.when(at < chips // 2)
                def _():
                    gone_ref[jnp.minimum(at, chips // 2 - 1)] = piece

                @pl.when(at >= chips // 2)
                def _():
                    kept_ref[jnp.maximum(at - chips // 2, 0)] = piece

    by_cols = ((rows, wide), lambda j, c: (0, j))
    piled = [sds((chips // 2, cut, width), BF16) for cut in cuts for _ in range(2)]
    active, back, cot, *piles = call(
        kernel,
        line,
        [normed, *pieces, up_here, view],
        [
            None,
            *[None] * n_cot,
            ((width, wide), lambda j, c: (0, j)),
            ((wide // block, None, block, width), lambda j, c: (j, c[CORE], 0, 0)),
        ],
        [
            sds((rows, hidden), BF16),
            sds((rows, hidden), BF16),
            sds((rows, width), BF16),
            *piled,
        ],
        [by_cols, by_cols, None, *[None] * len(piled)],
        (hidden // wide,),
        flops=6 * rows * hidden * width,
    )
    return active, back, cot, [piles[2 * n : 2 * n + 2] for n in range(len(cuts))]


def rows_gradient(line, sources, tasks, chips, cores, heads):
    rows = tasks[0][0][0].shape[0]
    width = sum(piece.shape[1] for piece in tasks[0][0])
    single = len(tasks) == 1
    widths = [right.shape[1] for _, right in tasks]
    wide = 512 if single and widths[0] % 512 == 0 else max(widths)
    steps = widths[0] // wide if single else len(tasks)
    per = width // (chips * cores)
    inputs, in_blocks = [], []
    for lefts, right in tasks:
        inputs += [*lefts, right]
        in_blocks += [*[None] * len(lefts), ((rows, wide), lambda j, c: (0, j)) if single else None]

    def kernel(here, *refs):
        gone_ref, kept_ref, turned_ref, tile_ref = refs[-4:]

        def turn(left_refs):
            column = 0
            for n, ref in enumerate(left_refs):
                size = ref.shape[1]
                to = column
                if len(left_refs) == 2:
                    to = pl.multiple_of(jnp.where(here[CORE] == n, 0, size), size)
                turned_ref[pl.ds(to, size), :] = jnp.transpose(ref[...])
                column += size

        def spread(columns, out_columns):
            for n in range(chips):
                number = here[sources + n]
                chip, head = number // heads, number % heads
                for k in range(cores):
                    start = pl.multiple_of(((chip * cores + k) * heads + head) * per, per)
                    ref = gone_ref if n < chips // 2 else kept_ref
                    ref[n % (chips // 2), k, :, out_columns] = tile_ref[pl.ds(start, per), columns]

        at, first = 0, 0
        for n, (lefts, right) in enumerate(tasks):
            left_refs, right_ref = refs[at : at + len(lefts)], refs[at + len(lefts)]
            at += len(lefts) + 1
            size = wide if single else widths[n]

            @pl.when(pl.program_id(0) == (0 if single else n))
            def _():
                turn(left_refs)

            @pl.when((pl.program_id(0) == n) | single)
            def _():
                tile_ref[:, :size] = dot(turned_ref[...], right_ref[...]).astype(BF16)
                spread(slice(0, size), slice(first, first + size))

            first += size

    total = sum(widths)
    block_columns = wide if single else total
    return call(
        kernel,
        line,
        inputs,
        in_blocks,
        [sds((chips // 2, cores, per, total), BF16)] * 2,
        [
            ((chips // 2, cores, per, block_columns), lambda j, c: (0, 0, 0, j if single else 0))
        ]
        * 2,
        (steps,),
        scratch=[pltpu.VMEM((width, rows), BF16), pltpu.VMEM((width, wide), BF16)],
        flops=2 * rows * width * total,
    )


def rows_gradient_whole(line, left, right):
    rows, width = left.shape
    columns = right.shape[1]
    wide = 512 if columns % 512 == 0 else columns

    def kernel(here, left_ref, right_ref, out_ref, turned_ref):
        @pl.when(pl.program_id(0) == 0)
        def _():
            turned_ref[...] = jnp.transpose(left_ref[...])

        out_ref[...] = dot(turned_ref[...], right_ref[...]).astype(BF16)

    return call(
        kernel,
        line,
        [left, right],
        [None, ((rows, wide), lambda j, c: (0, j))],
        [sds((width, columns), BF16)],
        [((width, wide), lambda j, c: (0, j))],
        (columns // wide,),
        scratch=[pltpu.VMEM((width, rows), BF16)],
        flops=2 * rows * width * columns,
    )[0]


def last_sums(line, sums):
    inputs, in_blocks, outs = [], [], []
    for parts, starts in sums:
        tail = parts[0].shape[1:]
        zeros = (0,) * len(tail)
        for part, at in zip(parts, starts):
            inputs.append(part)
            in_blocks.append(((1, *tail), lambda g, s, at=at, z=zeros: (s[at], *z)))
        outs += [sds(tail[1:], F32)] * 2 if len(tail) == 3 else [sds(tail, F32)]

    def kernel(here, *refs):
        ins, out_refs = refs[: len(inputs)], list(refs[len(inputs) :])
        first = 0
        for parts, _ in sums:
            mine = ins[first : first + len(parts)]
            first += len(parts)
            if parts[0].ndim == 4:
                for k in (here[CORE], 1 - here[CORE]):
                    out_refs.pop(0)[...] = sum(r[0, k].astype(F32) for r in mine)
            else:
                out_refs.pop(0)[...] = sum(r[0].astype(F32) for r in mine)

    return call(kernel, line, inputs, in_blocks, outs, [None] * len(outs), (1,))


def only_riders(line):
    call(lambda *_: None, line, [], [], [], [], (1,))


def place_columns(line, pairs_of, shapes, moves):
    def kernel(here, *refs):
        ins, outs = refs[: 2 * len(pairs_of)], refs[2 * len(pairs_of) :]
        c = here[CORE]
        for pair, first, wide, out, column0, column1 in moves:
            for turn in range(2):
                k = c if turn == 0 else 1 - c
                to = pl.multiple_of(column0 + k * (column1 - column0), wide)
                outs[out][:, pl.ds(to, wide)] = ins[2 * pair + turn][:, first : first + wide]

    inputs = [a for pair in pairs_of for a in pair]
    return call(
        kernel,
        line,
        inputs,
        [None] * len(inputs),
        [sds(s, F32) for s in shapes],
        [None] * len(shapes),
        (1,),
    )


def back_through(line, back, weight):
    rows, hidden = back.shape
    width = weight.shape[0]
    wide = 512

    def kernel(here, back_ref, w_ref, out_ref):
        out_ref[...] = dot(back_ref[...], w_ref[...], 1, 1).astype(BF16)

    return call(
        kernel,
        line,
        [back, weight],
        [None, ((wide, hidden), lambda n, c: (n, 0))],
        [sds((rows, width), BF16)],
        [((rows, wide), lambda n, c: (0, n))],
        (width // wide,),
        flops=2 * rows * hidden * width,
    )[0]


def project_down(line, active, weight, block):
    rows, hidden = active.shape
    width = weight.shape[1]
    half, wide = rows // 2, 512
    view = weight.reshape(hidden // block, 2, block, width)

    def kernel(here, active_ref, w_ref, own_ref, gone_ref):
        def part(which):
            place = pl.ds(pl.multiple_of(which * half, half), half)
            return dot(active_ref[place, :], w_ref[...].reshape(hidden, wide))

        gone_ref[...] = part(1 - here[CORE]).astype(BF16)
        own_ref[...] = part(here[CORE])

    by_cols = ((half, wide), lambda n, c: (0, n))
    return call(
        kernel,
        line,
        [active, view],
        [None, ((hidden // block, None, block, wide), lambda n, c: (0, c[CORE], 0, n))],
        [sds((half, width), F32), sds((half, width), BF16)],
        [by_cols, by_cols],
        (width // wide,),
        flops=2 * rows * hidden * width,
    )


def back_to_attended(line, grad_mine, grad_theirs, mid, cot, gain, weight):
    rows, width = mid.shape
    tall, part = 256, width // 2

    def kernel(here, gm_ref, gt_ref, mid_ref, cot_ref, gain_ref, w_ref, out_ref, cols_ref, mg_ref, gain_grad_ref):
        c = here[CORE]
        incoming = gm_ref[...].astype(F32) + gt_ref[...].astype(F32)
        centred, scale = moments(mid_ref[...])
        x_hat = centred * scale
        terms = incoming * x_hat
        scaled = incoming * gain_ref[...]
        mean_a = jnp.mean(scaled, axis=-1, keepdims=True)
        mean_b = jnp.mean(terms * gain_ref[...], axis=-1, keepdims=True)
        mid_grad = cot_ref[...].astype(F32) + scale * (scaled - mean_a - x_hat * mean_b)
        mg_ref[...] = mid_grad
        branch = mid_grad.astype(BF16)
        out_ref[...] = dot(branch, w_ref[pl.ds(pl.multiple_of(c * part, part), part), :], 1, 1).astype(BF16)
        cols_ref[...] = jnp.where(c == 0, branch[:, :part], branch[:, part:])

        @pl.when(pl.program_id(0) == 0)
        def _():
            gain_grad_ref[...] = jnp.zeros_like(gain_grad_ref)

        gain_grad_ref[...] += jnp.sum(terms.reshape(tall // 8, 8, width), axis=0)

    by_rows = ((tall, width), lambda i, c: (i, 0))
    half_rows = ((tall, part), lambda i, c: (i, 0))
    return call(
        kernel,
        line,
        [grad_mine, grad_theirs, mid, cot, gain, weight],
        [by_rows, by_rows, by_rows, by_rows, None, None],
        [
            sds((rows, part), BF16),
            sds((rows, part), BF16),
            sds((rows, width), F32),
            sds((8, width), F32),
        ],
        [half_rows, half_rows, by_rows, None],
        (rows // tall,),
        flops=rows * width * width,
    )


def back_through_qkv(line, backs, weight):
    rows = backs[0].shape[0]
    width, columns = weight.shape
    half, wide = rows // 2, 512

    def kernel(here, *refs):
        back_refs, (w_ref, own_ref, gone_ref) = refs[: len(backs)], refs[len(backs) :]

        def some(which):
            place = pl.ds(pl.multiple_of(which * half, half), half)
            total, first = 0.0, 0
            for ref in back_refs:
                last = first + ref.shape[1]
                total = total + dot(ref[place, :], w_ref[:, first:last], 1, 1)
                first = last
            return total

        gone_ref[...] = some(1 - here[CORE]).astype(BF16)
        own_ref[...] = some(here[CORE])

    by_cols = ((half, wide), lambda n, c: (0, n))
    return call(
        kernel,
        line,
        [*backs, weight],
        [*[None] * len(backs), ((wide, columns), lambda n, c: (n, 0))],
        [sds((half, width), F32), sds((half, width), BF16)],
        [by_cols, by_cols],
        (width // wide,),
        flops=2 * rows * columns * width,
    )


def back_to_tokens(line, grad_own, grad_came, toks, pass_embed, gain, mid_grad):
    half, width = grad_own.shape
    tall = 256
    steps = half // tall

    def kernel(here, own_ref, came_ref, toks_ref, pass_ref, gain_ref, mg_ref, out_ref, sums_ref):
        incoming = own_ref[...] + came_ref[...].astype(F32)
        centred, scale = moments(toks_ref[...].astype(F32) + pass_ref[...])
        x_hat = centred * scale
        terms = incoming * x_hat
        scaled = incoming * gain_ref[...]
        mean_a = jnp.mean(scaled, axis=-1, keepdims=True)
        mean_b = jnp.mean(terms * gain_ref[...], axis=-1, keepdims=True)
        resid_grad = mg_ref[...] + scale * (scaled - mean_a - x_hat * mean_b)
        out_ref[...] = resid_grad.astype(BF16)

        @pl.when(pl.program_id(0) == 0)
        def _():
            sums_ref[...] = jnp.zeros_like(sums_ref)

        sums_ref[0] += jnp.sum(resid_grad.reshape(tall // 8, 8, width), axis=0)
        sums_ref[1] += jnp.sum(terms.reshape(tall // 8, 8, width), axis=0)

    by_rows = ((tall, width), lambda i, c: (i, 0))
    own_rows = ((tall, width), lambda i, c: (c[CORE] * steps + i, 0))
    return call(
        kernel,
        line,
        [grad_own, grad_came, toks, pass_embed, gain, mid_grad],
        [by_rows, by_rows, own_rows, None, None, own_rows],
        [sds((half, width), BF16), sds((2, 8, width), F32)],
        [by_rows, None],
        (steps,),
        flops=20 * half * width,
    )


def body(
    sizes,
    tokens,
    seq_lengths,
    pass_embed,
    norm1_gain,
    qkv_weight,
    out_weight,
    norm2_gain,
    up_weight,
    down_weight,
    cotangent,
):
    n_chip, n_core, n_half, n_lane = sizes
    n_head = n_half * n_lane
    tok_rows, width = tokens.shape
    rows = 2 * tok_rows
    group_rows = tok_rows * n_head
    hidden = up_weight.shape[1]
    core = lax.axis_index("core")
    chip = lax.axis_index("chip")
    half = lax.axis_index("half")
    head = half * n_lane + lax.axis_index("lane")
    pass_row, gain1, gain2 = (v.reshape(1, width) for v in (pass_embed, norm1_gain, norm2_gain))

    def index(c, k, h, l):
        return ((c * n_core + k) * n_half + h) * n_lane + l

    everyone = [
        (c, k, h, l)
        for c in range(n_chip)
        for k in range(n_core)
        for h in range(n_half)
        for l in range(n_lane)
    ]
    def across_chip(pick):
        return [
            (index(c, k, h, l), index(c, 1 - k, h, l)) for c, k, h, l in everyone if pick(k, h)
        ]

    def stay(k, h):
        return k == h

    def leave(k, h):
        return k != h

    leavers = [d for d in everyone if leave(d[1], d[2])]
    regroup_perm = [(index(c, k, h, l), index(c, h, k, l)) for c, k, h, l in leavers]
    beside_perm = [(index(c, k, h, l), index(c, k, 1 - h, l)) for c, k, h, l in leavers]

    def send(value, pairs):
        return lax.ppermute(value, AXES, pairs)

    def regroup(value):
        return jnp.where(core == half, value, send(value, regroup_perm))

    def across(value):
        return lax.ppermute(value, "core", [(0, 1), (1, 0)])

    n_chips = n_chip * n_head
    n_bits = n_chips.bit_length() - 1
    number = chip * n_head + head
    bits = list(range(n_bits))
    near = ([0, 1, *bits[2:]], [1, 0, *bits[2:]])
    far_first = ([*bits[2:], 0, 1], [*bits[2:], 1, 0])

    tables, length = {}, 0

    def device_numbers(c, k, h, l):
        nonlocal length
        found = [k, h, int(k == h), 1 - h]
        me = c * n_head + h * n_lane + l
        for name, orders in (("near", near), ("far", far_first)):
            order = orders[k]
            mine = [(me >> b) & 1 for b in order]

            def pack(values):
                value = 0
                for v in values:
                    value = value * 2 + v
                return value

            def chip_at(place):
                values = [(place >> (n_bits - 1 - s)) & 1 for s in range(n_bits)]
                values[0] = mine[0] if values[0] else 1 - mine[0]
                return sum(v << b for v, b in zip(values, order))

            sources = [chip_at(p) for p in range(n_chips)]
            tables[name, "sources"] = len(found)
            found += sources
            tables[name, "places"] = len(found)
            found += [sources.index(n) for n in range(n_chips)]
            for step in range(1, n_bits):
                tables[name, step] = len(found)
                wanted = [*mine[:step], 1 - mine[step]]
                found += [pack(wanted[max(p, 1) :]) for p in range(step + 1)]
            tables[name, "last"] = len(found)
            found += [pack(mine[max(p, 1) :]) for p in range(n_bits + 1)]
        length = len(found)
        return found

    table = jnp.asarray([device_numbers(*d) for d in everyone], jnp.int32)
    here = lax.dynamic_slice(table, (lax.axis_index(AXES), 0), (1, length))[0]
    line = {"here": here, "turn": [], "sums": {}, "rides": {}, "after": [], "count": 0, "cost": COSTS}

    def flip(orders, step):
        def partner(c, k, h, l):
            other = (c * n_head + h * n_lane + l) ^ (1 << orders[k][step])
            return index(other // n_head, k, other % n_head // n_lane, other % n_lane)

        return [(index(*d), partner(*d)) for d in everyone]

    def sum_over_chips(name, gone, kept):
        orders = near if name == "near" else far_first
        parts = [kept]

        def send_blocks(arrays):
            parts.append(lax.ppermute(arrays[0], AXES, flip(orders, len(parts) - 1)))

        def starts():
            first = tables[name, "last" if len(parts) > n_bits else len(parts) - 1]
            return [first + p for p in range(len(parts))]

        def next_step():
            return list(parts), [(starts(), n_chips >> len(parts))]

        def advance():
            count = n_chips >> len(parts)
            send_blocks(
                [
                    sum(
                        lax.dynamic_slice_in_dim(p, here[at] * count, count, 0).astype(F32)
                        for p, at in zip(parts, starts())
                    ).astype(BF16)
                ]
            )

        def finish():
            while len(parts) <= n_bits:
                advance()
            return list(parts), starts()

        send_blocks([gone])
        return {"next_step": next_step, "send": send_blocks, "finish": finish}

    def split(whole, orders):
        view = whole.reshape((2,) * n_bits + whole.shape[1:])
        tail = tuple(range(n_bits, view.ndim))
        turned = [
            jnp.transpose(view, tuple(n_bits - 1 - b for b in o) + tail) for o in orders
        ]
        at = jnp.where(core == 0, (number >> orders[0][0]) & 1, (number >> orders[1][0]) & 1)

        def take(where):
            found = [lax.dynamic_index_in_dim(t, where, 0, keepdims=False) for t in turned]
            return jnp.where(core == 0, *found).reshape((n_chips // 2,) + whole.shape[1:])

        return take(1 - at), take(at)

    per = width // (n_chips * n_core)

    def gradient(name, *tasks):
        if per % 16 == 0:
            return rows_gradient(
                line, tables[name, "sources"], tasks, n_chips, n_core, n_head
            )
        wholes = []
        for lefts, right in tasks:
            left = lefts[0]
            if len(lefts) == 2:
                left = jnp.where(
                    core == 0, jnp.concatenate(lefts, axis=1), jnp.concatenate(lefts[::-1], axis=1)
                )
            wholes.append(rows_gradient_whole(line, left, right))
        whole = jnp.concatenate(wholes, axis=1)
        view = whole.reshape(n_chip, n_core, n_head, per, whole.shape[1])
        return split(jnp.swapaxes(view, 1, 2).reshape(n_chips, n_core, per, -1), near)

    part = width // 2
    ff_block = hidden // (n_chip * n_core)
    core_pairs = part // (2 * HEAD_DIM)
    stays = (core == half).astype(jnp.int32)

    def spread_group(value):
        near_came = send(value, across_chip(stay))
        leaver_came, stayer_came = send(value, regroup_perm), send(value, beside_perm)
        return [(value, near_came, (0, 0))], [(stayer_came, leaver_came, (1, 0))]

    near_toks, far_toks = spread_group(tokens)
    lengths_came = send(seq_lengths, across_chip(stay))
    qkv_here = qkv_columns(line, qkv_weight)
    first_half = project_qkv(
        line, HALF, [p[:2] for p in near_toks], pass_row, gain1, qkv_here
    )
    up_here = up_columns(line, up_weight, ff_block)
    near_cot, far_cot = spread_group(cotangent)
    toks, normed_a, qkv = project_qkv(
        line, OTHER_HALF, [p[:2] for p in far_toks], pass_row, gain1, qkv_here, first_half
    )
    lengths = jnp.where(core == half, seq_lengths, lengths_came)[0]
    order = jnp.arange(lengths.shape[0])
    ends = jnp.sum(jnp.where(order[:, None] <= order[None, :], lengths[:, None], 0), axis=0)

    def to_heads(value):
        value = lax.all_to_all(value, "lane", split_axis=1, concat_axis=0, tiled=True)
        value = value.reshape(n_lane, 2, tok_rows, -1)
        return jnp.swapaxes(value, 0, 1).reshape(group_rows, -1)

    def from_heads(value):
        value = value.reshape(2, n_lane, tok_rows, -1)
        value = jnp.swapaxes(value, 0, 1).reshape(group_rows, -1)
        return lax.all_to_all(value, "lane", split_axis=0, concat_axis=1, tiled=True)

    if n_lane > 1:
        qkv = to_heads(qkv)
    pairs = core_pairs // n_lane
    attended_heads, totals = attend(line, ends, qkv)
    mine = from_heads(attended_heads) if n_lane > 1 else attended_heads
    theirs = across(mine)

    line["after"] += [p for pair in far_cot for p in pair[:2]]
    middle, normed_m = project_out(
        line, mine, theirs, toks, pass_row, out_weight, gain2
    )
    per_ff = hidden // 2 // n_chips
    down_orders, cuts = ["near"], [per_ff]
    if per_ff % 32 == 0 and n_bits > 3:
        down_orders, cuts = ["far", "near"], [per_ff // 2] * 2
    active, upper_grad, cot, piles = feed_forward(
        line,
        [tables[name, "places"] for name in down_orders],
        normed_m,
        [*near_cot, *far_cot],
        up_here,
        down_weight,
        ff_block,
        n_chips,
        cuts,
    )
    down_sums = [sum_over_chips(o, *pile) for o, pile in zip(down_orders, piles)]
    normed_m_part = back_through(line, upper_grad, up_here)
    normed_m_came = across(normed_m_part)
    up_sum = sum_over_chips("near", *gradient("near", ([normed_m], upper_grad)))
    half_pairs = pairs if n_lane > 1 else max(1, pairs // 2)
    several = half_pairs < pairs and len(down_sums) > 1
    if several:
        line["rides"] = RIDES
        line["sums"] = {"a": down_sums[0], "b": down_sums[1], "u": up_sum}

    attended_grad, branch_cols, middle_grad, norm2_terms = back_to_attended(
        line, normed_m_part, normed_m_came, middle, cot, gain2, out_weight
    )
    if n_lane > 1:
        attended_grad = to_heads(attended_grad)

    def back_pairs(first):
        back = attend_back(
            line, ends, qkv, attended_heads, attended_grad, totals, first, half_pairs
        )
        return from_heads(back) if n_lane > 1 else back

    backs = [back_pairs(0)]
    rest_sums = [
        sum_over_chips("near",
            *gradient("near", ([normed_a], backs[0]), ([mine, theirs], branch_cols)),
        )
    ]
    line["sums"]["r"] = rest_sums[0]
    if half_pairs < pairs:
        backs.append(back_pairs(half_pairs))
        rest_sums.append(sum_over_chips("near", *gradient("near", ([normed_a], backs[1]))))
        line["sums"]["s"] = rest_sums[1]
    normed_a_own, normed_a_gone = back_through_qkv(line, backs, qkv_here)
    normed_a_came = across(normed_a_gone)
    output_own, output_gone = project_down(line, active, down_weight, ff_block)
    output_came = across(output_gone)
    token_grad, sums = back_to_tokens(
        line, normed_a_own, normed_a_came, toks, pass_row, gain1, middle_grad
    )
    token_grad = regroup(token_grad)
    if several:
        only_riders(line)
        only_riders(line)
    middle_own = lax.dynamic_slice_in_dim(middle, core * tok_rows, tok_rows, 0)
    mixed = regroup((middle_own + output_own + output_came.astype(F32)).astype(BF16))

    down_grad = jnp.concatenate(
        last_sums(line, [s["finish"]() for s in down_sums]), axis=0
    )
    up_own, up_gone = last_sums(line, [up_sum["finish"]()])
    up_pair = (up_own, across(up_gone))
    small = jnp.sum(jnp.concatenate([sums, 0.5 * norm2_terms[None]]), axis=1) + up_own[:1, :1] * 0
    n_all = len(everyone)
    small = jnp.swapaxes(small.reshape(3, n_all, width // n_all), 0, 1)
    small = lax.all_to_all(small, AXES, split_axis=0, concat_axis=0, tiled=True)
    small = jnp.sum(small, axis=0)
    line["after"] = [small]
    rest = last_sums(line, [s["finish"]() for s in rest_sums])
    pairs_of = [(rest[2 * n], across(rest[2 * n + 1])) for n in range(len(rest_sums))]
    (up_grad,) = place_columns(
        line,
        [up_pair],
        [(per, hidden)],
        [
            (0, n * ff_block, ff_block, 0, 2 * n * ff_block, (2 * n + 1) * ff_block)
            for n in range(n_chip)
        ],
    )
    size = 3 * part // len(rest_sums)
    moves = [(0, size, part, 0, 0, part)]
    two = 2 * HEAD_DIM
    for n in range(3):
        for lane in range(n_lane):
            for r in range(len(rest_sums)):
                for p in range(half_pairs):
                    first = ((lane * half_pairs + p) * 3 + n) * two
                    column = n * width + (lane * pairs + r * half_pairs + p) * two
                    moves.append((r, first, two, 1, column, column + part))
    out_grad, qkv_grad = place_columns(
        line, pairs_of, [(per, width), (per, 3 * width)], moves
    )

    return (
        mixed,
        token_grad,
        small[0],
        small[1],
        qkv_grad,
        out_grad,
        small[2],
        up_grad,
        down_grad,
    )


def solution(mesh):
    n_dp, n_head = mesh.shape["dp"], mesh.shape["head"]
    sizes = (n_dp // 2, 2, 2, n_head // 2)
    fine = Mesh(mesh.devices.reshape(sizes), AXES)
    rows, group = P(AXES), P(("chip", "core"))
    in_specs = (rows, group, P(), P(), P(), P(), P(), P(), P(), rows)
    return jax.shard_map(
        partial(body, sizes),
        mesh=fine,
        in_specs=in_specs,
        out_specs=(rows,) * 9,
        check_vma=False,
    )
```

```python
from functools import partial

import jax
import jax.numpy as jnp
from jax import lax
from jax.experimental import pallas as pl
from jax.experimental.pallas import tpu as pltpu
from jax.sharding import Mesh, PartitionSpec as P

HEADS = 16
HEAD_DIM = 64
AXES = ("chip", "core", "half", "lane")
F32 = jnp.float32
BF16 = jnp.bfloat16
COST = 20
COSTS = {9: 0.001, 8: 200, 2: 1, 17: 0.1, 0: 0.001, 1: 0.1, 18: 200, 7: 5, 5: 0.1, 14: 200, 15: 200, 6: 5, 13: 0.1, 4: 5}
RIDES = {10: 'ba', 12: 'bu', 13: 'r', 14: 'ba', 15: 'au', 16: 'rs', 17: 's', 18: 'u', 20: 'rs'}
SCORE_SCALE = HEAD_DIM**-0.5 * 1.4426950408889634
GELU_A, GELU_B = 0.7978845608028654, 0.044715


def call(kernel, line, inputs, in_blocks, out_shapes, out_blocks, grid, scratch=(), flops=0, aliases=None, more=()):
    (steps,) = grid
    n_in, n_out, body = len(inputs), len(out_shapes), kernel
    waits = [*line["turn"], *line["after"]]
    inputs, in_blocks = [*inputs, *waits], [*in_blocks, *["any"] * len(waits)]
    out_shapes, out_blocks = [*out_shapes, sds((8, 128), F32)], [*out_blocks, "any"]
    riders, works = [line["sums"][name] for name in line["rides"].get(line["count"], ())], []
    line["after"] = []
    for rider in riders:
        parts, wanted = rider["next_step"]()
        tail = parts[0].shape[1:]
        zeros = (0,) * len(tail)
        for starts, count in wanted:
            per = count // steps if count % steps == 0 else 1
            blocks = count // per
            works.append((rider, len(inputs), len(parts), len(out_shapes)))
            for part, at in zip(parts, starts, strict=True):
                inputs.append(part)
                in_blocks.append(
                    (
                        (per, *tail),
                        lambda g, s, at=at, b=blocks, z=zeros: (s[at] * b + jnp.minimum(g, b - 1), *z),
                    )
                )
            out_shapes.append(sds((count, *tail), BF16))
            out_blocks.append(
                ((per, *tail), lambda g, s, b=blocks, z=zeros: (jnp.minimum(g, b - 1), *z))
            )

    def kernel(*refs):
        numbers, refs = refs[: 1 + len(more)], refs[1 + len(more) :]
        ins, outs = refs[: len(inputs)], refs[len(inputs) : len(inputs) + len(out_shapes)]
        rest = refs[len(inputs) + len(out_shapes) :]
        body(*numbers, *ins[:n_in], *outs[:n_out], *rest)
        for _, first, width, out in works:
            outs[out][...] = sum(r[...].astype(F32) for r in ins[first : first + width]).astype(BF16)

    def spec(array, block):
        if block is None:
            rank = len(array.shape)
            return pl.BlockSpec(array.shape, lambda *_: (0,) * rank)
        if block == "any":
            return pl.BlockSpec(memory_space=pl.ANY)
        return pl.BlockSpec(block[0], lambda g, s, *_: block[1](g, s))

    moved = sum(a.size * a.dtype.itemsize for a in (*inputs, *out_shapes))
    weight = line["cost"].get(line["count"], COST)
    line["count"] += 1
    outs = pl.pallas_call(
        kernel,
        out_shape=out_shapes,
        grid_spec=pltpu.PrefetchScalarGridSpec(
            num_scalar_prefetch=1 + len(more),
            grid=grid,
            in_specs=[spec(a, b) for a, b in zip(inputs, in_blocks, strict=True)],
            out_specs=[spec(a, b) for a, b in zip(out_shapes, out_blocks, strict=True)],
            scratch_shapes=list(scratch),
        ),
        compiler_params=pltpu.CompilerParams(vmem_limit_bytes=56 * 2**20),
        cost_estimate=pl.CostEstimate(
            flops=int(flops * weight), bytes_accessed=int(moved * weight), transcendentals=0
        ),
        input_output_aliases={k + len(more): v for k, v in (aliases or {}).items()},
    )(line["here"], *more, *inputs)
    line["turn"] = [outs[n_out]]
    for rider in riders:
        rider["send"]([outs[out] for who, _, _, out in works if who is rider])
    return list(outs[:n_out])


def sds(shape, dtype):
    return jax.ShapeDtypeStruct(shape, dtype)


def moments(hidden):
    row_mean = jnp.mean(hidden, axis=-1, keepdims=True)
    centred = hidden - row_mean
    variance = jnp.mean(centred * centred, axis=-1, keepdims=True)
    return centred, lax.rsqrt(variance + 1e-05)


def dot(a, b, ca=1, cb=0):
    return lax.dot_general(a, b, (((ca,), (cb,)), ((), ())), preferred_element_type=F32)


CORE, HALF, STAYS, OTHER_HALF, TABLES = range(5)


def qkv_columns(line, weight):
    width = weight.shape[0]
    tall, two = 256, 2 * HEAD_DIM
    pairs = width // 2 // two

    def kernel(here, in_ref, out_ref):
        for p in range(pairs):
            for t in range(3):
                start = pl.multiple_of(t * width + here[CORE] * (width // 2) + p * two, two)
                to = (3 * p + t) * two
                out_ref[:, to : to + two] = in_ref[:, pl.ds(start, two)]

    return copy_rows(line, kernel, weight, tall)


def up_columns(line, weight, block):
    hidden = weight.shape[1]

    def kernel(here, in_ref, out_ref):
        for n in range(hidden // 2 // block):
            start = pl.multiple_of((2 * n + here[CORE]) * block, block)
            out_ref[:, n * block : (n + 1) * block] = in_ref[:, pl.ds(start, block)]

    return copy_rows(line, kernel, weight, 256)


def copy_rows(line, kernel, weight, tall):
    rows, columns = weight.shape

    def by_rows(wide):
        return ((tall, wide), lambda i, c: (i, 0))

    return call(
        kernel,
        line,
        [weight],
        [by_rows(columns)],
        [sds((rows, columns // 2), BF16)],
        [by_rows(columns // 2)],
        (rows // tall,),
    )[0]


def copy_picked(stays, pairs, copy):
    for here, came, row in pairs:
        @pl.when(stays == 1)
        def _():
            copy(here, row)

        @pl.when(stays != 1)
        def _():
            copy(came, row)


def project_qkv(line, at, pairs, pass_embed, gain, weight, into=None):
    pieces = [p for pair in pairs for p in pair]
    width = pieces[0].shape[1]
    heights = [min(piece.shape[0] for piece in pair) for pair in pairs]
    half = sum(heights)
    rows, wide = 2 * half, 512
    columns = weight.shape[1]

    def kernel(here, *refs):
        piece_refs, (pass_ref, gain_ref, w_ref, *refs) = refs[: len(pieces)], refs[len(pieces) :]
        toks_ref, normed_ref, qkv_ref = refs[-3:]

        def norm_rows(ref, row):
            for start in range(0, ref.shape[0], 64):
                low = ref[start : start + 64, :]
                centred, scale = moments(low.astype(F32) + pass_ref[...])
                to = slice(row + start, row + start + 64)
                toks_ref[to, :] = low
                normed_ref[to, :] = (centred * scale * gain_ref[...]).astype(BF16)

        @pl.when(pl.program_id(0) == 0)
        def _():
            firsts = [sum(heights[:n]) for n in range(len(pairs))]
            copy_picked(
                here[STAYS],
                [(piece_refs[2 * n], piece_refs[2 * n + 1], f) for n, f in enumerate(firsts)],
                norm_rows,
            )

        qkv_ref[...] = dot(normed_ref[...], w_ref[...]).astype(BF16)

    inputs = [*pieces, pass_embed, gain, weight]
    in_blocks = [((h, width), lambda j, a: (0, 0)) for h in heights for _ in range(2)]
    in_blocks += [None, None, ((width, wide), lambda j, a: (0, j))]
    aliases = {}
    if into is not None:
        aliases = {len(inputs) + 1 + n: n for n in range(3)}
        inputs += into
        in_blocks += ["any"] * 3
    all_rows = ((half, width), lambda j, a: (a[at], 0))
    return call(
        kernel,
        line,
        inputs,
        in_blocks,
        [sds((rows, width), BF16), sds((rows, width), BF16), sds((rows, columns), BF16)],
        [all_rows, all_rows, ((half, wide), lambda j, a: (a[at], j))],
        (columns // wide,),
        flops=rows * width * columns,
        aliases=aliases,
    )


def allowed(first_key, first_query, keys, queries, ends, diagonal):
    at_query = first_query + lax.broadcasted_iota(jnp.int32, (1, queries), 1)
    start = jnp.zeros_like(at_query)
    for end in ends:
        start = jnp.where(at_query >= end, end, start)
    at_key = first_key + lax.broadcasted_iota(jnp.int32, (keys, queries), 0)
    mask = at_key >= start
    if diagonal:
        mask = mask & (at_key <= at_query)
    return mask


def attention_block(group_rows):
    return 256 if group_rows <= 1024 else 512


def attend(line, ends, qkv):
    group_rows, columns = qkv.shape
    pairs = columns // (6 * HEAD_DIM)
    step = attention_block(group_rows)
    n_ends = ends.shape[0]

    def kernel(here, ends_ref, qkv_ref, o_ref, total_ref, vt_ref):
        q_ref, k_ref, v_ref = (qkv_ref.at[:, pl.ds(2 * HEAD_DIM * n, 2 * HEAD_DIM)] for n in range(3))
        bounds = [ends_ref[n] for n in range(n_ends)]
        vt_ref[...] = jnp.transpose(v_ref[...])
        lane = lax.broadcasted_iota(jnp.int32, (1, 2 * HEAD_DIM), 1)
        for i in range(group_rows // step):
            rows = slice(i * step, (i + 1) * step)
            outs = []
            masks = [
                allowed(j * step, i * step, step, step, bounds, j == i) for j in range(i + 1)
            ]
            for h in range(2):
                q = jnp.where(lane // HEAD_DIM == h, q_ref[rows, :], 0)
                scores = [
                    jnp.where(
                        masks[j],
                        dot(k_ref[j * step : (j + 1) * step, :], q, 1, 1) * SCORE_SCALE,
                        -1e30,
                    )
                    for j in range(i + 1)
                ]
                top = jnp.max(scores[0], axis=0, keepdims=True)
                for s in scores[1:]:
                    top = jnp.maximum(top, jnp.max(s, axis=0, keepdims=True))
                total = jnp.zeros_like(top)
                out = jnp.zeros((HEAD_DIM, step), F32)
                for j in range(i + 1):
                    p = jnp.exp2(scores[j] - top)
                    total = total + jnp.sum(p, axis=0, keepdims=True)
                    out = out + dot(
                        vt_ref[h * HEAD_DIM : (h + 1) * HEAD_DIM, j * step : (j + 1) * step],
                        p.astype(BF16),
                    )
                outs.append(out * (1.0 / total))
                total_ref[0, h : h + 1, rows] = top + jnp.log2(total)
            o_ref[rows, :] = jnp.transpose(jnp.concatenate(outs, axis=0)).astype(BF16)

    block = (group_rows, 2 * HEAD_DIM)
    return call(
        kernel,
        line,
        [qkv],
        [((group_rows, 6 * HEAD_DIM), lambda p, e: (0, p))],
        [
            sds((group_rows, pairs * 2 * HEAD_DIM), BF16),
            sds((pairs, 2, group_rows), F32),
        ],
        [(block, lambda p, e: (0, p)), ((1, 2, group_rows), lambda p, e: (p, 0, 0))],
        (pairs,),
        scratch=[pltpu.VMEM((2 * HEAD_DIM, group_rows), BF16)],
        flops=pairs * 4 * group_rows * group_rows * 2 * HEAD_DIM,
        more=[ends],
    )


def attend_back(line, ends, qkv, attended, attended_grad, totals, first, pairs):
    group_rows = qkv.shape[0]
    step = attention_block(group_rows)
    n_ends = ends.shape[0]

    def kernel(here, ends_ref, qkv_ref, o_ref, g_ref, total_ref, out_ref, dk_acc, dv_acc):
        q_ref, k_ref, v_ref = (qkv_ref.at[:, pl.ds(2 * HEAD_DIM * n, 2 * HEAD_DIM)] for n in range(3))
        bounds = [ends_ref[n] for n in range(n_ends)]
        lane = lax.broadcasted_iota(jnp.int32, (1, 2 * HEAD_DIM), 1)
        for i in range(group_rows // step):
            rows = slice(i * step, (i + 1) * step)
            products = jnp.transpose(g_ref[rows, :].astype(F32) * o_ref[rows, :].astype(F32))
            masks = [
                allowed(j * step, i * step, step, step, bounds, j == i) for j in range(i + 1)
            ]
            dq = jnp.zeros((step, 2 * HEAD_DIM), F32)
            for h in range(2):
                here = lane // HEAD_DIM == h
                q = jnp.where(here, q_ref[rows, :], 0)
                g = jnp.where(here, g_ref[rows, :], 0)
                delta = jnp.sum(products[h * HEAD_DIM : (h + 1) * HEAD_DIM], axis=0, keepdims=True)
                total = total_ref[0, h : h + 1, rows]
                for j in range(i + 1):
                    keys = slice(j * step, (j + 1) * step)
                    k = k_ref[keys, :]
                    scores = jnp.where(masks[j], dot(k, q, 1, 1) * SCORE_SCALE, -1e30)
                    p = jnp.exp2(scores - total)
                    back = (p * (dot(v_ref[keys, :], g, 1, 1) - delta)).astype(BF16)
                    dv = dot(p.astype(BF16), g)
                    dk = dot(back, q)
                    if j == i and h == 0:
                        dv_acc[keys, :] = dv
                        dk_acc[keys, :] = dk
                    else:
                        dv_acc[keys, :] += dv
                        dk_acc[keys, :] += dk
                    dq = dq + dot(back, jnp.where(here, k, 0), 0, 0)
            out_ref[rows, : 2 * HEAD_DIM] = (dq * HEAD_DIM**-0.5).astype(BF16)
        out_ref[:, 2 * HEAD_DIM : 4 * HEAD_DIM] = (dk_acc[...] * HEAD_DIM**-0.5).astype(BF16)
        out_ref[:, 4 * HEAD_DIM :] = dv_acc[...].astype(BF16)

    block = (group_rows, 2 * HEAD_DIM)
    return call(
        kernel,
        line,
        [qkv, attended, attended_grad, totals],
        [
            ((group_rows, 6 * HEAD_DIM), lambda p, e: (0, first + p)),
            (block, lambda p, e: (0, first + p)),
            (block, lambda p, e: (0, first + p)),
            ((1, 2, group_rows), lambda p, e: (first + p, 0, 0)),
        ],
        [sds((group_rows, pairs * 6 * HEAD_DIM), BF16)],
        [((group_rows, 6 * HEAD_DIM), lambda p, e: (0, p))],
        (pairs,),
        scratch=[pltpu.VMEM(block, F32), pltpu.VMEM(block, F32)],
        flops=pairs * 10 * group_rows * group_rows * 2 * HEAD_DIM,
        more=[ends],
    )[0]


def project_out(line, mine, theirs, toks, pass_embed, weight, gain):
    rows, width = toks.shape
    tall, part = 256, width // 2

    def kernel(here, mine_ref, theirs_ref, toks_ref, pass_ref, w_ref, gain_ref, mid_ref, normed_ref):
        def weight_rows(which):
            return w_ref[pl.ds(pl.multiple_of(which * part, part), part), :]

        mid = (
            toks_ref[...].astype(F32)
            + pass_ref[...]
            + dot(mine_ref[...], weight_rows(here[CORE]))
            + dot(theirs_ref[...], weight_rows(1 - here[CORE]))
        )
        mid_ref[...] = mid
        centred, scale = moments(mid)
        normed_ref[...] = (centred * scale * gain_ref[...]).astype(BF16)

    by_rows = ((tall, width), lambda i, c: (i, 0))
    half_rows = ((tall, part), lambda i, c: (i, 0))
    return call(
        kernel,
        line,
        [mine, theirs, toks, pass_embed, weight, gain],
        [half_rows, half_rows, by_rows, None, None, None],
        [sds((rows, width), F32), sds((rows, width), BF16)],
        [by_rows, by_rows],
        (rows // tall,),
        flops=2 * rows * width * width,
    )


def feed_forward(line, places, normed, cot_pairs, up_here, down_weight, block, chips, cuts):
    pieces = [p for pair in cot_pairs for p in pair[:2]]
    firsts = [pair[2] for pair in cot_pairs]
    width = normed.shape[1]
    rows, wide = normed.shape[0], 512
    half = rows // 2
    hidden = up_here.shape[1]
    per = hidden // chips
    many = wide // per
    view = down_weight.reshape(hidden // block, 2, block, width)
    n_cot = len(pieces)

    def kernel(here, normed_ref, *refs):
        cot_refs = refs[:n_cot]
        up_ref, down_ref, active_ref, back_ref, cot_ref, *piles = refs[n_cot:]
        j = pl.program_id(0)

        def copy(ref, place):
            far, row = place
            start = here[HALF if far == 0 else OTHER_HALF] * half + row
            cot_ref[pl.ds(pl.multiple_of(start, 16), ref.shape[0]), :] = ref[...]

        @pl.when(j == 0)
        def _():
            copy_picked(
                here[STAYS],
                [(cot_refs[2 * n], cot_refs[2 * n + 1], f) for n, f in enumerate(firsts)],
                copy,
            )

        upper = dot(normed_ref[...], up_ref[...])
        square = upper * upper
        bend = jnp.tanh(upper * (GELU_A + (GELU_A * GELU_B) * square))
        rise = 0.5 + 0.5 * bend
        active = (upper * rise).astype(BF16)
        active_ref[...] = active
        slope = 0.5 * GELU_A + (1.5 * GELU_A * GELU_B) * square
        steep = rise + upper * (slope * (1.0 - bend * bend))
        down = down_ref[...].reshape(wide, width)
        back_ref[...] = (dot(cot_ref[...], down, 1, 1) * steep).astype(BF16)
        grad = dot(active, cot_ref[...], 0, 0).astype(BF16)
        for r in range(many):
            row = r * per
            for n, cut in enumerate(cuts):
                piece = grad[row : row + cut]
                row += cut
                at = here[places[n] + j * many + r]
                gone_ref, kept_ref = piles[2 * n : 2 * n + 2]

                @pl.when(at < chips // 2)
                def _():
                    gone_ref[jnp.minimum(at, chips // 2 - 1)] = piece

                @pl.when(at >= chips // 2)
                def _():
                    kept_ref[jnp.maximum(at - chips // 2, 0)] = piece

    by_cols = ((rows, wide), lambda j, c: (0, j))
    piled = [sds((chips // 2, cut, width), BF16) for cut in cuts for _ in range(2)]
    active, back, cot, *piles = call(
        kernel,
        line,
        [normed, *pieces, up_here, view],
        [
            None,
            *[None] * n_cot,
            ((width, wide), lambda j, c: (0, j)),
            ((wide // block, None, block, width), lambda j, c: (j, c[CORE], 0, 0)),
        ],
        [
            sds((rows, hidden), BF16),
            sds((rows, hidden), BF16),
            sds((rows, width), BF16),
            *piled,
        ],
        [by_cols, by_cols, None, *[None] * len(piled)],
        (hidden // wide,),
        flops=6 * rows * hidden * width,
    )
    return active, back, cot, [piles[2 * n : 2 * n + 2] for n in range(len(cuts))]


def rows_gradient(line, sources, tasks, chips, cores, heads):
    rows = tasks[0][0][0].shape[0]
    width = sum(piece.shape[1] for piece in tasks[0][0])
    single = len(tasks) == 1
    widths = [right.shape[1] for _, right in tasks]
    wide = 512 if single and widths[0] % 512 == 0 else max(widths)
    steps = widths[0] // wide if single else len(tasks)
    per = width // (chips * cores)
    inputs, in_blocks = [], []
    for lefts, right in tasks:
        inputs += [*lefts, right]
        in_blocks += [*[None] * len(lefts), ((rows, wide), lambda j, c: (0, j)) if single else None]

    def kernel(here, *refs):
        gone_ref, kept_ref, turned_ref, tile_ref = refs[-4:]

        def turn(left_refs):
            column = 0
            for n, ref in enumerate(left_refs):
                size = ref.shape[1]
                to = column
                if len(left_refs) == 2:
                    to = pl.multiple_of(jnp.where(here[CORE] == n, 0, size), size)
                turned_ref[pl.ds(to, size), :] = jnp.transpose(ref[...])
                column += size

        def spread(columns, out_columns):
            for n in range(chips):
                number = here[sources + n]
                chip, head = number // heads, number % heads
                for k in range(cores):
                    start = pl.multiple_of(((chip * cores + k) * heads + head) * per, per)
                    ref = gone_ref if n < chips // 2 else kept_ref
                    ref[n % (chips // 2), k, :, out_columns] = tile_ref[pl.ds(start, per), columns]

        at, first = 0, 0
        for n, (lefts, right) in enumerate(tasks):
            left_refs, right_ref = refs[at : at + len(lefts)], refs[at + len(lefts)]
            at += len(lefts) + 1
            size = wide if single else widths[n]

            @pl.when(pl.program_id(0) == (0 if single else n))
            def _():
                turn(left_refs)

            @pl.when((pl.program_id(0) == n) | single)
            def _():
                tile_ref[:, :size] = dot(turned_ref[...], right_ref[...]).astype(BF16)
                spread(slice(0, size), slice(first, first + size))

            first += size

    total = sum(widths)
    block_columns = wide if single else total
    return call(
        kernel,
        line,
        inputs,
        in_blocks,
        [sds((chips // 2, cores, per, total), BF16)] * 2,
        [
            ((chips // 2, cores, per, block_columns), lambda j, c: (0, 0, 0, j if single else 0))
        ]
        * 2,
        (steps,),
        scratch=[pltpu.VMEM((width, rows), BF16), pltpu.VMEM((width, wide), BF16)],
        flops=2 * rows * width * total,
    )


def rows_gradient_whole(line, left, right):
    rows, width = left.shape
    columns = right.shape[1]
    wide = 512 if columns % 512 == 0 else columns

    def kernel(here, left_ref, right_ref, out_ref, turned_ref):
        @pl.when(pl.program_id(0) == 0)
        def _():
            turned_ref[...] = jnp.transpose(left_ref[...])

        out_ref[...] = dot(turned_ref[...], right_ref[...]).astype(BF16)

    return call(
        kernel,
        line,
        [left, right],
        [None, ((rows, wide), lambda j, c: (0, j))],
        [sds((width, columns), BF16)],
        [((width, wide), lambda j, c: (0, j))],
        (columns // wide,),
        scratch=[pltpu.VMEM((width, rows), BF16)],
        flops=2 * rows * width * columns,
    )[0]


def last_sums(line, sums):
    inputs, in_blocks, outs = [], [], []
    for parts, starts in sums:
        tail = parts[0].shape[1:]
        zeros = (0,) * len(tail)
        for part, at in zip(parts, starts):
            inputs.append(part)
            in_blocks.append(((1, *tail), lambda g, s, at=at, z=zeros: (s[at], *z)))
        outs += [sds(tail[1:], F32)] * 2 if len(tail) == 3 else [sds(tail, F32)]

    def kernel(here, *refs):
        ins, out_refs = refs[: len(inputs)], list(refs[len(inputs) :])
        first = 0
        for parts, _ in sums:
            mine = ins[first : first + len(parts)]
            first += len(parts)
            if parts[0].ndim == 4:
                for k in (here[CORE], 1 - here[CORE]):
                    out_refs.pop(0)[...] = sum(r[0, k].astype(F32) for r in mine)
            else:
                out_refs.pop(0)[...] = sum(r[0].astype(F32) for r in mine)

    return call(kernel, line, inputs, in_blocks, outs, [None] * len(outs), (1,))


def only_riders(line):
    call(lambda *_: None, line, [], [], [], [], (1,))


def place_columns(line, pairs_of, shapes, moves):
    def kernel(here, *refs):
        ins, outs = refs[: 2 * len(pairs_of)], refs[2 * len(pairs_of) :]
        c = here[CORE]
        for pair, first, wide, out, column0, column1 in moves:
            for turn in range(2):
                k = c if turn == 0 else 1 - c
                to = pl.multiple_of(column0 + k * (column1 - column0), wide)
                outs[out][:, pl.ds(to, wide)] = ins[2 * pair + turn][:, first : first + wide]

    inputs = [a for pair in pairs_of for a in pair]
    return call(
        kernel,
        line,
        inputs,
        [None] * len(inputs),
        [sds(s, F32) for s in shapes],
        [None] * len(shapes),
        (1,),
    )


def back_through(line, back, weight):
    rows, hidden = back.shape
    width = weight.shape[0]
    wide = 512

    def kernel(here, back_ref, w_ref, out_ref):
        out_ref[...] = dot(back_ref[...], w_ref[...], 1, 1).astype(BF16)

    return call(
        kernel,
        line,
        [back, weight],
        [None, ((wide, hidden), lambda n, c: (n, 0))],
        [sds((rows, width), BF16)],
        [((rows, wide), lambda n, c: (0, n))],
        (width // wide,),
        flops=2 * rows * hidden * width,
    )[0]


def project_down(line, active, weight, block):
    rows, hidden = active.shape
    width = weight.shape[1]
    half, wide = rows // 2, 512
    view = weight.reshape(hidden // block, 2, block, width)

    def kernel(here, active_ref, w_ref, own_ref, gone_ref):
        def part(which):
            place = pl.ds(pl.multiple_of(which * half, half), half)
            return dot(active_ref[place, :], w_ref[...].reshape(hidden, wide))

        gone_ref[...] = part(1 - here[CORE]).astype(BF16)
        own_ref[...] = part(here[CORE])

    by_cols = ((half, wide), lambda n, c: (0, n))
    return call(
        kernel,
        line,
        [active, view],
        [None, ((hidden // block, None, block, wide), lambda n, c: (0, c[CORE], 0, n))],
        [sds((half, width), F32), sds((half, width), BF16)],
        [by_cols, by_cols],
        (width // wide,),
        flops=2 * rows * hidden * width,
    )


def back_to_attended(line, grad_mine, grad_theirs, mid, cot, gain, weight):
    rows, width = mid.shape
    tall, part = 256, width // 2

    def kernel(here, gm_ref, gt_ref, mid_ref, cot_ref, gain_ref, w_ref, out_ref, cols_ref, mg_ref, gain_grad_ref):
        c = here[CORE]
        incoming = gm_ref[...].astype(F32) + gt_ref[...].astype(F32)
        centred, scale = moments(mid_ref[...])
        x_hat = centred * scale
        terms = incoming * x_hat
        scaled = incoming * gain_ref[...]
        mean_a = jnp.mean(scaled, axis=-1, keepdims=True)
        mean_b = jnp.mean(terms * gain_ref[...], axis=-1, keepdims=True)
        mid_grad = cot_ref[...].astype(F32) + scale * (scaled - mean_a - x_hat * mean_b)
        mg_ref[...] = mid_grad
        branch = mid_grad.astype(BF16)
        out_ref[...] = dot(branch, w_ref[pl.ds(pl.multiple_of(c * part, part), part), :], 1, 1).astype(BF16)
        cols_ref[...] = jnp.where(c == 0, branch[:, :part], branch[:, part:])

        @pl.when(pl.program_id(0) == 0)
        def _():
            gain_grad_ref[...] = jnp.zeros_like(gain_grad_ref)

        gain_grad_ref[...] += jnp.sum(terms.reshape(tall // 8, 8, width), axis=0)

    by_rows = ((tall, width), lambda i, c: (i, 0))
    half_rows = ((tall, part), lambda i, c: (i, 0))
    return call(
        kernel,
        line,
        [grad_mine, grad_theirs, mid, cot, gain, weight],
        [by_rows, by_rows, by_rows, by_rows, None, None],
        [
            sds((rows, part), BF16),
            sds((rows, part), BF16),
            sds((rows, width), F32),
            sds((8, width), F32),
        ],
        [half_rows, half_rows, by_rows, None],
        (rows // tall,),
        flops=rows * width * width,
    )


def back_through_qkv(line, backs, weight):
    rows = backs[0].shape[0]
    width, columns = weight.shape
    half, wide = rows // 2, 512

    def kernel(here, *refs):
        back_refs, (w_ref, own_ref, gone_ref) = refs[: len(backs)], refs[len(backs) :]

        def some(which):
            place = pl.ds(pl.multiple_of(which * half, half), half)
            total, first = 0.0, 0
            for ref in back_refs:
                last = first + ref.shape[1]
                total = total + dot(ref[place, :], w_ref[:, first:last], 1, 1)
                first = last
            return total

        gone_ref[...] = some(1 - here[CORE]).astype(BF16)
        own_ref[...] = some(here[CORE])

    by_cols = ((half, wide), lambda n, c: (0, n))
    return call(
        kernel,
        line,
        [*backs, weight],
        [*[None] * len(backs), ((wide, columns), lambda n, c: (n, 0))],
        [sds((half, width), F32), sds((half, width), BF16)],
        [by_cols, by_cols],
        (width // wide,),
        flops=2 * rows * columns * width,
    )


def back_to_tokens(line, grad_own, grad_came, toks, pass_embed, gain, mid_grad):
    half, width = grad_own.shape
    tall = 256
    steps = half // tall

    def kernel(here, own_ref, came_ref, toks_ref, pass_ref, gain_ref, mg_ref, out_ref, sums_ref):
        incoming = own_ref[...] + came_ref[...].astype(F32)
        centred, scale = moments(toks_ref[...].astype(F32) + pass_ref[...])
        x_hat = centred * scale
        terms = incoming * x_hat
        scaled = incoming * gain_ref[...]
        mean_a = jnp.mean(scaled, axis=-1, keepdims=True)
        mean_b = jnp.mean(terms * gain_ref[...], axis=-1, keepdims=True)
        resid_grad = mg_ref[...] + scale * (scaled - mean_a - x_hat * mean_b)
        out_ref[...] = resid_grad.astype(BF16)

        @pl.when(pl.program_id(0) == 0)
        def _():
            sums_ref[...] = jnp.zeros_like(sums_ref)

        sums_ref[0] += jnp.sum(resid_grad.reshape(tall // 8, 8, width), axis=0)
        sums_ref[1] += jnp.sum(terms.reshape(tall // 8, 8, width), axis=0)

    by_rows = ((tall, width), lambda i, c: (i, 0))
    own_rows = ((tall, width), lambda i, c: (c[CORE] * steps + i, 0))
    return call(
        kernel,
        line,
        [grad_own, grad_came, toks, pass_embed, gain, mid_grad],
        [by_rows, by_rows, own_rows, None, None, own_rows],
        [sds((half, width), BF16), sds((2, 8, width), F32)],
        [by_rows, None],
        (steps,),
        flops=20 * half * width,
    )


def body(
    sizes,
    tokens,
    seq_lengths,
    pass_embed,
    norm1_gain,
    qkv_weight,
    out_weight,
    norm2_gain,
    up_weight,
    down_weight,
    cotangent,
):
    n_chip, n_core, n_half, n_lane = sizes
    n_head = n_half * n_lane
    tok_rows, width = tokens.shape
    rows = 2 * tok_rows
    group_rows = tok_rows * n_head
    hidden = up_weight.shape[1]
    core = lax.axis_index("core")
    chip = lax.axis_index("chip")
    half = lax.axis_index("half")
    head = half * n_lane + lax.axis_index("lane")
    pass_row, gain1, gain2 = (v.reshape(1, width) for v in (pass_embed, norm1_gain, norm2_gain))

    def index(c, k, h, l):
        return ((c * n_core + k) * n_half + h) * n_lane + l

    everyone = [
        (c, k, h, l)
        for c in range(n_chip)
        for k in range(n_core)
        for h in range(n_half)
        for l in range(n_lane)
    ]
    def across_chip(pick):
        return [
            (index(c, k, h, l), index(c, 1 - k, h, l)) for c, k, h, l in everyone if pick(k, h)
        ]

    def stay(k, h):
        return k == h

    def leave(k, h):
        return k != h

    leavers = [d for d in everyone if leave(d[1], d[2])]
    regroup_perm = [(index(c, k, h, l), index(c, h, k, l)) for c, k, h, l in leavers]
    beside_perm = [(index(c, k, h, l), index(c, k, 1 - h, l)) for c, k, h, l in leavers]

    def send(value, pairs):
        return lax.ppermute(value, AXES, pairs)

    def regroup(value):
        return jnp.where(core == half, value, send(value, regroup_perm))

    def across(value):
        return lax.ppermute(value, "core", [(0, 1), (1, 0)])

    n_chips = n_chip * n_head
    n_bits = n_chips.bit_length() - 1
    number = chip * n_head + head
    bits = list(range(n_bits))
    near = ([0, 1, *bits[2:]], [1, 0, *bits[2:]])
    far_first = ([*bits[2:], 0, 1], [*bits[2:], 1, 0])

    tables, length = {}, 0

    def device_numbers(c, k, h, l):
        nonlocal length
        found = [k, h, int(k == h), 1 - h]
        me = c * n_head + h * n_lane + l
        for name, orders in (("near", near), ("far", far_first)):
            order = orders[k]
            mine = [(me >> b) & 1 for b in order]

            def pack(values):
                value = 0
                for v in values:
                    value = value * 2 + v
                return value

            def chip_at(place):
                values = [(place >> (n_bits - 1 - s)) & 1 for s in range(n_bits)]
                values[0] = mine[0] if values[0] else 1 - mine[0]
                return sum(v << b for v, b in zip(values, order))

            sources = [chip_at(p) for p in range(n_chips)]
            tables[name, "sources"] = len(found)
            found += sources
            tables[name, "places"] = len(found)
            found += [sources.index(n) for n in range(n_chips)]
            for step in range(1, n_bits):
                tables[name, step] = len(found)
                wanted = [*mine[:step], 1 - mine[step]]
                found += [pack(wanted[max(p, 1) :]) for p in range(step + 1)]
            tables[name, "last"] = len(found)
            found += [pack(mine[max(p, 1) :]) for p in range(n_bits + 1)]
        length = len(found)
        return found

    table = jnp.asarray([device_numbers(*d) for d in everyone], jnp.int32)
    here = lax.dynamic_slice(table, (lax.axis_index(AXES), 0), (1, length))[0]
    line = {"here": here, "turn": [], "sums": {}, "rides": {}, "after": [], "count": 0, "cost": COSTS}

    def flip(orders, step):
        def partner(c, k, h, l):
            other = (c * n_head + h * n_lane + l) ^ (1 << orders[k][step])
            return index(other // n_head, k, other % n_head // n_lane, other % n_lane)

        return [(index(*d), partner(*d)) for d in everyone]

    def sum_over_chips(name, gone, kept):
        orders = near if name == "near" else far_first
        parts = [kept]

        def send_blocks(arrays):
            parts.append(lax.ppermute(arrays[0], AXES, flip(orders, len(parts) - 1)))

        def starts():
            first = tables[name, "last" if len(parts) > n_bits else len(parts) - 1]
            return [first + p for p in range(len(parts))]

        def next_step():
            return list(parts), [(starts(), n_chips >> len(parts))]

        def advance():
            count = n_chips >> len(parts)
            send_blocks(
                [
                    sum(
                        lax.dynamic_slice_in_dim(p, here[at] * count, count, 0).astype(F32)
                        for p, at in zip(parts, starts())
                    ).astype(BF16)
                ]
            )

        def finish():
            while len(parts) <= n_bits:
                advance()
            return list(parts), starts()

        send_blocks([gone])
        return {"next_step": next_step, "send": send_blocks, "finish": finish}

    def split(whole, orders):
        view = whole.reshape((2,) * n_bits + whole.shape[1:])
        tail = tuple(range(n_bits, view.ndim))
        turned = [
            jnp.transpose(view, tuple(n_bits - 1 - b for b in o) + tail) for o in orders
        ]
        at = jnp.where(core == 0, (number >> orders[0][0]) & 1, (number >> orders[1][0]) & 1)

        def take(where):
            found = [lax.dynamic_index_in_dim(t, where, 0, keepdims=False) for t in turned]
            return jnp.where(core == 0, *found).reshape((n_chips // 2,) + whole.shape[1:])

        return take(1 - at), take(at)

    per = width // (n_chips * n_core)

    def gradient(name, *tasks):
        if per % 16 == 0:
            return rows_gradient(
                line, tables[name, "sources"], tasks, n_chips, n_core, n_head
            )
        wholes = []
        for lefts, right in tasks:
            left = lefts[0]
            if len(lefts) == 2:
                left = jnp.where(
                    core == 0, jnp.concatenate(lefts, axis=1), jnp.concatenate(lefts[::-1], axis=1)
                )
            wholes.append(rows_gradient_whole(line, left, right))
        whole = jnp.concatenate(wholes, axis=1)
        view = whole.reshape(n_chip, n_core, n_head, per, whole.shape[1])
        return split(jnp.swapaxes(view, 1, 2).reshape(n_chips, n_core, per, -1), near)

    part = width // 2
    ff_block = hidden // (n_chip * n_core)
    core_pairs = part // (2 * HEAD_DIM)
    stays = (core == half).astype(jnp.int32)

    def spread_group(value):
        near_came = send(value, across_chip(stay))
        leaver_came, stayer_came = send(value, regroup_perm), send(value, beside_perm)
        return [(value, near_came, (0, 0))], [(stayer_came, leaver_came, (1, 0))]

    near_toks, far_toks = spread_group(tokens)
    lengths_came = send(seq_lengths, across_chip(stay))
    qkv_here = qkv_columns(line, qkv_weight)
    first_half = project_qkv(
        line, HALF, [p[:2] for p in near_toks], pass_row, gain1, qkv_here
    )
    up_here = up_columns(line, up_weight, ff_block)
    near_cot, far_cot = spread_group(cotangent)
    toks, normed_a, qkv = project_qkv(
        line, OTHER_HALF, [p[:2] for p in far_toks], pass_row, gain1, qkv_here, first_half
    )
    lengths = jnp.where(core == half, seq_lengths, lengths_came)[0]
    order = jnp.arange(lengths.shape[0])
    ends = jnp.sum(jnp.where(order[:, None] <= order[None, :], lengths[:, None], 0), axis=0)

    def to_heads(value):
        value = lax.all_to_all(value, "lane", split_axis=1, concat_axis=0, tiled=True)
        value = value.reshape(n_lane, 2, tok_rows, -1)
        return jnp.swapaxes(value, 0, 1).reshape(group_rows, -1)

    def from_heads(value):
        value = value.reshape(2, n_lane, tok_rows, -1)
        value = jnp.swapaxes(value, 0, 1).reshape(group_rows, -1)
        return lax.all_to_all(value, "lane", split_axis=0, concat_axis=1, tiled=True)

    if n_lane > 1:
        qkv = to_heads(qkv)
    pairs = core_pairs // n_lane
    attended_heads, totals = attend(line, ends, qkv)
    mine = from_heads(attended_heads) if n_lane > 1 else attended_heads
    theirs = across(mine)

    line["after"] += [p for pair in far_cot for p in pair[:2]]
    middle, normed_m = project_out(
        line, mine, theirs, toks, pass_row, out_weight, gain2
    )
    per_ff = hidden // 2 // n_chips
    down_orders, cuts = ["near"], [per_ff]
    if per_ff % 32 == 0 and n_bits > 3:
        down_orders, cuts = ["far", "near"], [per_ff // 2] * 2
    active, upper_grad, cot, piles = feed_forward(
        line,
        [tables[name, "places"] for name in down_orders],
        normed_m,
        [*near_cot, *far_cot],
        up_here,
        down_weight,
        ff_block,
        n_chips,
        cuts,
    )
    down_sums = [sum_over_chips(o, *pile) for o, pile in zip(down_orders, piles)]
    normed_m_part = back_through(line, upper_grad, up_here)
    normed_m_came = across(normed_m_part)
    up_sum = sum_over_chips("near", *gradient("near", ([normed_m], upper_grad)))
    half_pairs = pairs if n_lane > 1 else max(1, pairs // 2)
    several = half_pairs < pairs and len(down_sums) > 1
    if several:
        line["rides"] = RIDES
        line["sums"] = {"a": down_sums[0], "b": down_sums[1], "u": up_sum}

    attended_grad, branch_cols, middle_grad, norm2_terms = back_to_attended(
        line, normed_m_part, normed_m_came, middle, cot, gain2, out_weight
    )
    if n_lane > 1:
        attended_grad = to_heads(attended_grad)

    def back_pairs(first):
        back = attend_back(
            line, ends, qkv, attended_heads, attended_grad, totals, first, half_pairs
        )
        return from_heads(back) if n_lane > 1 else back

    backs = [back_pairs(0)]
    rest_sums = [
        sum_over_chips("near",
            *gradient("near", ([normed_a], backs[0]), ([mine, theirs], branch_cols)),
        )
    ]
    line["sums"]["r"] = rest_sums[0]
    if half_pairs < pairs:
        backs.append(back_pairs(half_pairs))
        rest_sums.append(sum_over_chips("near", *gradient("near", ([normed_a], backs[1]))))
        line["sums"]["s"] = rest_sums[1]
    normed_a_own, normed_a_gone = back_through_qkv(line, backs, qkv_here)
    normed_a_came = across(normed_a_gone)
    output_own, output_gone = project_down(line, active, down_weight, ff_block)
    output_came = across(output_gone)
    token_grad, sums = back_to_tokens(
        line, normed_a_own, normed_a_came, toks, pass_row, gain1, middle_grad
    )
    token_grad = regroup(token_grad)
    if several:
        only_riders(line)
        only_riders(line)
    middle_own = lax.dynamic_slice_in_dim(middle, core * tok_rows, tok_rows, 0)
    mixed = regroup((middle_own + output_own + output_came.astype(F32)).astype(BF16))

    down_grad = jnp.concatenate(
        last_sums(line, [s["finish"]() for s in down_sums]), axis=0
    )
    up_own, up_gone = last_sums(line, [up_sum["finish"]()])
    up_pair = (up_own, across(up_gone))
    (up_grad,) = place_columns(
        line,
        [up_pair],
        [(per, hidden)],
        [
            (0, n * ff_block, ff_block, 0, 2 * n * ff_block, (2 * n + 1) * ff_block)
            for n in range(n_chip)
        ],
    )
    small = jnp.sum(jnp.concatenate([sums, 0.5 * norm2_terms[None]]), axis=1) + up_grad[:1, :1] * 0
    n_all = len(everyone)
    small = jnp.swapaxes(small.reshape(3, n_all, width // n_all), 0, 1)
    small = lax.all_to_all(small, AXES, split_axis=0, concat_axis=0, tiled=True)
    small = jnp.sum(small, axis=0)
    rest = last_sums(line, [s["finish"]() for s in rest_sums])
    pairs_of = [(rest[2 * n], across(rest[2 * n + 1])) for n in range(len(rest_sums))]
    size = 3 * part // len(rest_sums)
    moves = [(0, size, part, 0, 0, part)]
    two = 2 * HEAD_DIM
    for n in range(3):
        for lane in range(n_lane):
            for r in range(len(rest_sums)):
                for p in range(half_pairs):
                    first = ((lane * half_pairs + p) * 3 + n) * two
                    column = n * width + (lane * pairs + r * half_pairs + p) * two
                    moves.append((r, first, two, 1, column, column + part))
    line["after"] = [small]
    out_grad, qkv_grad = place_columns(
        line, pairs_of, [(per, width), (per, 3 * width)], moves
    )

    return (
        mixed,
        token_grad,
        small[0],
        small[1],
        qkv_grad,
        out_grad,
        small[2],
        up_grad,
        down_grad,
    )


def solution(mesh):
    n_dp, n_head = mesh.shape["dp"], mesh.shape["head"]
    sizes = (n_dp // 2, 2, 2, n_head // 2)
    fine = Mesh(mesh.devices.reshape(sizes), AXES)
    rows, group = P(AXES), P(("chip", "core"))
    in_specs = (rows, group, P(), P(), P(), P(), P(), P(), P(), rows)
    return jax.shard_map(
        partial(body, sizes),
        mesh=fine,
        in_specs=in_specs,
        out_specs=(rows,) * 9,
        check_vma=False,
    )
```

```python
from functools import partial

import jax
import jax.numpy as jnp
from jax import lax
from jax.experimental import pallas as pl
from jax.experimental.pallas import tpu as pltpu
from jax.sharding import Mesh, PartitionSpec as P

HEADS = 16
HEAD_DIM = 64
AXES = ("chip", "core", "half", "lane")
F32 = jnp.float32
BF16 = jnp.bfloat16
COST = 20
COSTS = {9: 0.001, 8: 200, 2: 1, 17: 0.1, 0: 0.001, 1: 0.1, 18: 200, 7: 5, 5: 0.1, 14: 200, 15: 200, 6: 5, 13: 0.1, 4: 5}
RIDES = {10: 'ba', 12: 'bu', 13: 'r', 14: 'ba', 15: 'au', 16: 'rs', 17: 's', 18: 'u', 20: 'rs'}
SCORE_SCALE = HEAD_DIM**-0.5 * 1.4426950408889634
GELU_A, GELU_B = 0.7978845608028654, 0.044715


def call(kernel, line, inputs, in_blocks, out_shapes, out_blocks, grid, scratch=(), flops=0, aliases=None, more=()):
    (steps,) = grid
    n_in, n_out, body = len(inputs), len(out_shapes), kernel
    waits = [*line["turn"], *line["after"]]
    inputs, in_blocks = [*inputs, *waits], [*in_blocks, *["any"] * len(waits)]
    out_shapes, out_blocks = [*out_shapes, sds((8, 128), F32)], [*out_blocks, "any"]
    riders, works = [line["sums"][name] for name in line["rides"].get(line["count"], ())], []
    line["after"] = []
    for rider in riders:
        parts, wanted = rider["next_step"]()
        tail = parts[0].shape[1:]
        zeros = (0,) * len(tail)
        for starts, count in wanted:
            per = count // steps if count % steps == 0 else 1
            blocks = count // per
            works.append((rider, len(inputs), len(parts), len(out_shapes)))
            for part, at in zip(parts, starts, strict=True):
                inputs.append(part)
                in_blocks.append(
                    (
                        (per, *tail),
                        lambda g, s, at=at, b=blocks, z=zeros: (s[at] * b + jnp.minimum(g, b - 1), *z),
                    )
                )
            out_shapes.append(sds((count, *tail), BF16))
            out_blocks.append(
                ((per, *tail), lambda g, s, b=blocks, z=zeros: (jnp.minimum(g, b - 1), *z))
            )

    def kernel(*refs):
        numbers, refs = refs[: 1 + len(more)], refs[1 + len(more) :]
        ins, outs = refs[: len(inputs)], refs[len(inputs) : len(inputs) + len(out_shapes)]
        rest = refs[len(inputs) + len(out_shapes) :]
        body(*numbers, *ins[:n_in], *outs[:n_out], *rest)
        for _, first, width, out in works:
            outs[out][...] = sum(r[...].astype(F32) for r in ins[first : first + width]).astype(BF16)

    def spec(array, block):
        if block is None:
            rank = len(array.shape)
            return pl.BlockSpec(array.shape, lambda *_: (0,) * rank)
        if block == "any":
            return pl.BlockSpec(memory_space=pl.ANY)
        return pl.BlockSpec(block[0], lambda g, s, *_: block[1](g, s))

    moved = sum(a.size * a.dtype.itemsize for a in (*inputs, *out_shapes))
    weight = line["cost"].get(line["count"], COST)
    line["count"] += 1
    outs = pl.pallas_call(
        kernel,
        out_shape=out_shapes,
        grid_spec=pltpu.PrefetchScalarGridSpec(
            num_scalar_prefetch=1 + len(more),
            grid=grid,
            in_specs=[spec(a, b) for a, b in zip(inputs, in_blocks, strict=True)],
            out_specs=[spec(a, b) for a, b in zip(out_shapes, out_blocks, strict=True)],
            scratch_shapes=list(scratch),
        ),
        compiler_params=pltpu.CompilerParams(vmem_limit_bytes=63 * 2**20),
        cost_estimate=pl.CostEstimate(
            flops=int(flops * weight), bytes_accessed=int(moved * weight), transcendentals=0
        ),
        input_output_aliases={k + len(more): v for k, v in (aliases or {}).items()},
    )(line["here"], *more, *inputs)
    line["turn"] = [outs[n_out]]
    for rider in riders:
        rider["send"]([outs[out] for who, _, _, out in works if who is rider])
    return list(outs[:n_out])


def sds(shape, dtype):
    return jax.ShapeDtypeStruct(shape, dtype)


def moments(hidden):
    row_mean = jnp.mean(hidden, axis=-1, keepdims=True)
    centred = hidden - row_mean
    variance = jnp.mean(centred * centred, axis=-1, keepdims=True)
    return centred, lax.rsqrt(variance + 1e-05)


def dot(a, b, ca=1, cb=0):
    return lax.dot_general(a, b, (((ca,), (cb,)), ((), ())), preferred_element_type=F32)


CORE, HALF, STAYS, OTHER_HALF, TABLES = range(5)


def qkv_columns(line, weight):
    width = weight.shape[0]
    tall, two = 256, 2 * HEAD_DIM
    pairs = width // 2 // two

    def kernel(here, in_ref, out_ref):
        for p in range(pairs):
            for t in range(3):
                start = pl.multiple_of(t * width + here[CORE] * (width // 2) + p * two, two)
                to = (3 * p + t) * two
                out_ref[:, to : to + two] = in_ref[:, pl.ds(start, two)]

    return copy_rows(line, kernel, weight, tall)


def up_columns(line, weight, block):
    hidden = weight.shape[1]

    def kernel(here, in_ref, out_ref):
        for n in range(hidden // 2 // block):
            start = pl.multiple_of((2 * n + here[CORE]) * block, block)
            out_ref[:, n * block : (n + 1) * block] = in_ref[:, pl.ds(start, block)]

    return copy_rows(line, kernel, weight, 256)


def copy_rows(line, kernel, weight, tall):
    rows, columns = weight.shape

    def by_rows(wide):
        return ((tall, wide), lambda i, c: (i, 0))

    return call(
        kernel,
        line,
        [weight],
        [by_rows(columns)],
        [sds((rows, columns // 2), BF16)],
        [by_rows(columns // 2)],
        (rows // tall,),
    )[0]


def copy_picked(stays, pairs, copy):
    for here, came, row in pairs:
        @pl.when(stays == 1)
        def _():
            copy(here, row)

        @pl.when(stays != 1)
        def _():
            copy(came, row)


def project_qkv(line, at, pairs, pass_embed, gain, weight, into=None):
    pieces = [p for pair in pairs for p in pair]
    width = pieces[0].shape[1]
    heights = [min(piece.shape[0] for piece in pair) for pair in pairs]
    half = sum(heights)
    rows, wide = 2 * half, 512
    columns = weight.shape[1]

    def kernel(here, *refs):
        piece_refs, (pass_ref, gain_ref, w_ref, *refs) = refs[: len(pieces)], refs[len(pieces) :]
        toks_ref, normed_ref, qkv_ref = refs[-3:]

        def norm_rows(ref, row):
            for start in range(0, ref.shape[0], 64):
                low = ref[start : start + 64, :]
                centred, scale = moments(low.astype(F32) + pass_ref[...])
                to = slice(row + start, row + start + 64)
                toks_ref[to, :] = low
                normed_ref[to, :] = (centred * scale * gain_ref[...]).astype(BF16)

        @pl.when(pl.program_id(0) == 0)
        def _():
            firsts = [sum(heights[:n]) for n in range(len(pairs))]
            copy_picked(
                here[STAYS],
                [(piece_refs[2 * n], piece_refs[2 * n + 1], f) for n, f in enumerate(firsts)],
                norm_rows,
            )

        qkv_ref[...] = dot(normed_ref[...], w_ref[...]).astype(BF16)

    inputs = [*pieces, pass_embed, gain, weight]
    in_blocks = [((h, width), lambda j, a: (0, 0)) for h in heights for _ in range(2)]
    in_blocks += [None, None, ((width, wide), lambda j, a: (0, j))]
    aliases = {}
    if into is not None:
        aliases = {len(inputs) + 1 + n: n for n in range(3)}
        inputs += into
        in_blocks += ["any"] * 3
    all_rows = ((half, width), lambda j, a: (a[at], 0))
    return call(
        kernel,
        line,
        inputs,
        in_blocks,
        [sds((rows, width), BF16), sds((rows, width), BF16), sds((rows, columns), BF16)],
        [all_rows, all_rows, ((half, wide), lambda j, a: (a[at], j))],
        (columns // wide,),
        flops=rows * width * columns,
        aliases=aliases,
    )


def allowed(first_key, first_query, keys, queries, ends, diagonal):
    at_query = first_query + lax.broadcasted_iota(jnp.int32, (1, queries), 1)
    start = jnp.zeros_like(at_query)
    for end in ends:
        start = jnp.where(at_query >= end, end, start)
    at_key = first_key + lax.broadcasted_iota(jnp.int32, (keys, queries), 0)
    mask = at_key >= start
    if diagonal:
        mask = mask & (at_key <= at_query)
    return mask


def attention_block(group_rows):
    return 256 if group_rows <= 1024 else 512


def attend(line, ends, qkv):
    group_rows, columns = qkv.shape
    pairs = columns // (6 * HEAD_DIM)
    step = attention_block(group_rows)
    n_ends = ends.shape[0]

    def kernel(here, ends_ref, qkv_ref, o_ref, total_ref, vt_ref):
        q_ref, k_ref, v_ref = (qkv_ref.at[:, pl.ds(2 * HEAD_DIM * n, 2 * HEAD_DIM)] for n in range(3))
        bounds = [ends_ref[n] for n in range(n_ends)]
        vt_ref[...] = jnp.transpose(v_ref[...])
        lane = lax.broadcasted_iota(jnp.int32, (1, 2 * HEAD_DIM), 1)
        for i in range(group_rows // step):
            rows = slice(i * step, (i + 1) * step)
            outs = []
            masks = [
                allowed(j * step, i * step, step, step, bounds, j == i) for j in range(i + 1)
            ]
            for h in range(2):
                q = jnp.where(lane // HEAD_DIM == h, q_ref[rows, :], 0)
                scores = [
                    jnp.where(
                        masks[j],
                        dot(k_ref[j * step : (j + 1) * step, :], q, 1, 1) * SCORE_SCALE,
                        -1e30,
                    )
                    for j in range(i + 1)
                ]
                top = jnp.max(scores[0], axis=0, keepdims=True)
                for s in scores[1:]:
                    top = jnp.maximum(top, jnp.max(s, axis=0, keepdims=True))
                total = jnp.zeros_like(top)
                out = jnp.zeros((HEAD_DIM, step), F32)
                for j in range(i + 1):
                    p = jnp.exp2(scores[j] - top)
                    total = total + jnp.sum(p, axis=0, keepdims=True)
                    out = out + dot(
                        vt_ref[h * HEAD_DIM : (h + 1) * HEAD_DIM, j * step : (j + 1) * step],
                        p.astype(BF16),
                    )
                outs.append(out * (1.0 / total))
                total_ref[0, h : h + 1, rows] = top + jnp.log2(total)
            o_ref[rows, :] = jnp.transpose(jnp.concatenate(outs, axis=0)).astype(BF16)

    block = (group_rows, 2 * HEAD_DIM)
    return call(
        kernel,
        line,
        [qkv],
        [((group_rows, 6 * HEAD_DIM), lambda p, e: (0, p))],
        [
            sds((group_rows, pairs * 2 * HEAD_DIM), BF16),
            sds((pairs, 2, group_rows), F32),
        ],
        [(block, lambda p, e: (0, p)), ((1, 2, group_rows), lambda p, e: (p, 0, 0))],
        (pairs,),
        scratch=[pltpu.VMEM((2 * HEAD_DIM, group_rows), BF16)],
        flops=pairs * 4 * group_rows * group_rows * 2 * HEAD_DIM,
        more=[ends],
    )


def attend_back(line, ends, qkv, attended, attended_grad, totals, first, pairs):
    group_rows = qkv.shape[0]
    step = attention_block(group_rows)
    n_ends = ends.shape[0]

    def kernel(here, ends_ref, qkv_ref, o_ref, g_ref, total_ref, out_ref, dk_acc, dv_acc):
        q_ref, k_ref, v_ref = (qkv_ref.at[:, pl.ds(2 * HEAD_DIM * n, 2 * HEAD_DIM)] for n in range(3))
        bounds = [ends_ref[n] for n in range(n_ends)]
        lane = lax.broadcasted_iota(jnp.int32, (1, 2 * HEAD_DIM), 1)
        for i in range(group_rows // step):
            rows = slice(i * step, (i + 1) * step)
            products = jnp.transpose(g_ref[rows, :].astype(F32) * o_ref[rows, :].astype(F32))
            masks = [
                allowed(j * step, i * step, step, step, bounds, j == i) for j in range(i + 1)
            ]
            dq = jnp.zeros((step, 2 * HEAD_DIM), F32)
            for h in range(2):
                here = lane // HEAD_DIM == h
                q = jnp.where(here, q_ref[rows, :], 0)
                g = jnp.where(here, g_ref[rows, :], 0)
                delta = jnp.sum(products[h * HEAD_DIM : (h + 1) * HEAD_DIM], axis=0, keepdims=True)
                total = total_ref[0, h : h + 1, rows]
                for j in range(i + 1):
                    keys = slice(j * step, (j + 1) * step)
                    k = k_ref[keys, :]
                    scores = jnp.where(masks[j], dot(k, q, 1, 1) * SCORE_SCALE, -1e30)
                    p = jnp.exp2(scores - total)
                    back = (p * (dot(v_ref[keys, :], g, 1, 1) - delta)).astype(BF16)
                    dv = dot(p.astype(BF16), g)
                    dk = dot(back, q)
                    if j == i and h == 0:
                        dv_acc[keys, :] = dv
                        dk_acc[keys, :] = dk
                    else:
                        dv_acc[keys, :] += dv
                        dk_acc[keys, :] += dk
                    dq = dq + dot(back, jnp.where(here, k, 0), 0, 0)
            out_ref[rows, : 2 * HEAD_DIM] = (dq * HEAD_DIM**-0.5).astype(BF16)
        out_ref[:, 2 * HEAD_DIM : 4 * HEAD_DIM] = (dk_acc[...] * HEAD_DIM**-0.5).astype(BF16)
        out_ref[:, 4 * HEAD_DIM :] = dv_acc[...].astype(BF16)

    block = (group_rows, 2 * HEAD_DIM)
    return call(
        kernel,
        line,
        [qkv, attended, attended_grad, totals],
        [
            ((group_rows, 6 * HEAD_DIM), lambda p, e: (0, first + p)),
            (block, lambda p, e: (0, first + p)),
            (block, lambda p, e: (0, first + p)),
            ((1, 2, group_rows), lambda p, e: (first + p, 0, 0)),
        ],
        [sds((group_rows, pairs * 6 * HEAD_DIM), BF16)],
        [((group_rows, 6 * HEAD_DIM), lambda p, e: (0, p))],
        (pairs,),
        scratch=[pltpu.VMEM(block, F32), pltpu.VMEM(block, F32)],
        flops=pairs * 10 * group_rows * group_rows * 2 * HEAD_DIM,
        more=[ends],
    )[0]


def project_out(line, mine, theirs, toks, pass_embed, weight, gain):
    rows, width = toks.shape
    tall, part = 256, width // 2

    def kernel(here, mine_ref, theirs_ref, toks_ref, pass_ref, w_ref, gain_ref, mid_ref, normed_ref):
        def weight_rows(which):
            return w_ref[pl.ds(pl.multiple_of(which * part, part), part), :]

        mid = (
            toks_ref[...].astype(F32)
            + pass_ref[...]
            + dot(mine_ref[...], weight_rows(here[CORE]))
            + dot(theirs_ref[...], weight_rows(1 - here[CORE]))
        )
        mid_ref[...] = mid
        centred, scale = moments(mid)
        normed_ref[...] = (centred * scale * gain_ref[...]).astype(BF16)

    by_rows = ((tall, width), lambda i, c: (i, 0))
    half_rows = ((tall, part), lambda i, c: (i, 0))
    return call(
        kernel,
        line,
        [mine, theirs, toks, pass_embed, weight, gain],
        [half_rows, half_rows, by_rows, None, None, None],
        [sds((rows, width), F32), sds((rows, width), BF16)],
        [by_rows, by_rows],
        (rows // tall,),
        flops=2 * rows * width * width,
    )


def feed_forward(line, places, normed, cot_pairs, up_here, down_weight, block, chips, cuts):
    pieces = [p for pair in cot_pairs for p in pair[:2]]
    firsts = [pair[2] for pair in cot_pairs]
    width = normed.shape[1]
    rows, wide = normed.shape[0], 512
    half = rows // 2
    hidden = up_here.shape[1]
    per = hidden // chips
    many = wide // per
    view = down_weight.reshape(hidden // block, 2, block, width)
    n_cot = len(pieces)

    def kernel(here, normed_ref, *refs):
        cot_refs = refs[:n_cot]
        up_ref, down_ref, active_ref, back_ref, cot_ref, *piles = refs[n_cot:]
        j = pl.program_id(0)

        def copy(ref, place):
            far, row = place
            start = here[HALF if far == 0 else OTHER_HALF] * half + row
            cot_ref[pl.ds(pl.multiple_of(start, 16), ref.shape[0]), :] = ref[...]

        @pl.when(j == 0)
        def _():
            copy_picked(
                here[STAYS],
                [(cot_refs[2 * n], cot_refs[2 * n + 1], f) for n, f in enumerate(firsts)],
                copy,
            )

        upper = dot(normed_ref[...], up_ref[...])
        square = upper * upper
        bend = jnp.tanh(upper * (GELU_A + (GELU_A * GELU_B) * square))
        rise = 0.5 + 0.5 * bend
        active = (upper * rise).astype(BF16)
        active_ref[...] = active
        slope = 0.5 * GELU_A + (1.5 * GELU_A * GELU_B) * square
        steep = rise + upper * (slope * (1.0 - bend * bend))
        down = down_ref[...].reshape(wide, width)
        back_ref[...] = (dot(cot_ref[...], down, 1, 1) * steep).astype(BF16)
        grad = dot(active, cot_ref[...], 0, 0).astype(BF16)
        for r in range(many):
            row = r * per
            for n, cut in enumerate(cuts):
                piece = grad[row : row + cut]
                row += cut
                at = here[places[n] + j * many + r]
                gone_ref, kept_ref = piles[2 * n : 2 * n + 2]

                @pl.when(at < chips // 2)
                def _():
                    gone_ref[jnp.minimum(at, chips // 2 - 1)] = piece

                @pl.when(at >= chips // 2)
                def _():
                    kept_ref[jnp.maximum(at - chips // 2, 0)] = piece

    by_cols = ((rows, wide), lambda j, c: (0, j))
    piled = [sds((chips // 2, cut, width), BF16) for cut in cuts for _ in range(2)]
    active, back, cot, *piles = call(
        kernel,
        line,
        [normed, *pieces, up_here, view],
        [
            None,
            *[None] * n_cot,
            ((width, wide), lambda j, c: (0, j)),
            ((wide // block, None, block, width), lambda j, c: (j, c[CORE], 0, 0)),
        ],
        [
            sds((rows, hidden), BF16),
            sds((rows, hidden), BF16),
            sds((rows, width), BF16),
            *piled,
        ],
        [by_cols, by_cols, None, *[None] * len(piled)],
        (hidden // wide,),
        flops=6 * rows * hidden * width,
    )
    return active, back, cot, [piles[2 * n : 2 * n + 2] for n in range(len(cuts))]


def rows_gradient(line, sources, tasks, chips, cores, heads):
    rows = tasks[0][0][0].shape[0]
    width = sum(piece.shape[1] for piece in tasks[0][0])
    single = len(tasks) == 1
    widths = [right.shape[1] for _, right in tasks]
    wide = 512 if single and widths[0] % 512 == 0 else max(widths)
    steps = widths[0] // wide if single else len(tasks)
    per = width // (chips * cores)
    inputs, in_blocks = [], []
    for lefts, right in tasks:
        inputs += [*lefts, right]
        in_blocks += [*[None] * len(lefts), ((rows, wide), lambda j, c: (0, j)) if single else None]

    def kernel(here, *refs):
        gone_ref, kept_ref, turned_ref, tile_ref = refs[-4:]

        def turn(left_refs):
            column = 0
            for n, ref in enumerate(left_refs):
                size = ref.shape[1]
                to = column
                if len(left_refs) == 2:
                    to = pl.multiple_of(jnp.where(here[CORE] == n, 0, size), size)
                turned_ref[pl.ds(to, size), :] = jnp.transpose(ref[...])
                column += size

        def spread(columns, out_columns):
            for n in range(chips):
                number = here[sources + n]
                chip, head = number // heads, number % heads
                for k in range(cores):
                    start = pl.multiple_of(((chip * cores + k) * heads + head) * per, per)
                    ref = gone_ref if n < chips // 2 else kept_ref
                    ref[n % (chips // 2), k, :, out_columns] = tile_ref[pl.ds(start, per), columns]

        at, first = 0, 0
        for n, (lefts, right) in enumerate(tasks):
            left_refs, right_ref = refs[at : at + len(lefts)], refs[at + len(lefts)]
            at += len(lefts) + 1
            size = wide if single else widths[n]

            @pl.when(pl.program_id(0) == (0 if single else n))
            def _():
                turn(left_refs)

            @pl.when((pl.program_id(0) == n) | single)
            def _():
                tile_ref[:, :size] = dot(turned_ref[...], right_ref[...]).astype(BF16)
                spread(slice(0, size), slice(first, first + size))

            first += size

    total = sum(widths)
    block_columns = wide if single else total
    return call(
        kernel,
        line,
        inputs,
        in_blocks,
        [sds((chips // 2, cores, per, total), BF16)] * 2,
        [
            ((chips // 2, cores, per, block_columns), lambda j, c: (0, 0, 0, j if single else 0))
        ]
        * 2,
        (steps,),
        scratch=[pltpu.VMEM((width, rows), BF16), pltpu.VMEM((width, wide), BF16)],
        flops=2 * rows * width * total,
    )


def rows_gradient_whole(line, left, right):
    rows, width = left.shape
    columns = right.shape[1]
    wide = 512 if columns % 512 == 0 else columns

    def kernel(here, left_ref, right_ref, out_ref, turned_ref):
        @pl.when(pl.program_id(0) == 0)
        def _():
            turned_ref[...] = jnp.transpose(left_ref[...])

        out_ref[...] = dot(turned_ref[...], right_ref[...]).astype(BF16)

    return call(
        kernel,
        line,
        [left, right],
        [None, ((rows, wide), lambda j, c: (0, j))],
        [sds((width, columns), BF16)],
        [((width, wide), lambda j, c: (0, j))],
        (columns // wide,),
        scratch=[pltpu.VMEM((width, rows), BF16)],
        flops=2 * rows * width * columns,
    )[0]


def last_sums(line, sums):
    inputs, in_blocks, outs = [], [], []
    for parts, starts in sums:
        tail = parts[0].shape[1:]
        zeros = (0,) * len(tail)
        for part, at in zip(parts, starts):
            inputs.append(part)
            in_blocks.append(((1, *tail), lambda g, s, at=at, z=zeros: (s[at], *z)))
        outs += [sds(tail[1:], F32)] * 2 if len(tail) == 3 else [sds(tail, F32)]

    def kernel(here, *refs):
        ins, out_refs = refs[: len(inputs)], list(refs[len(inputs) :])
        first = 0
        for parts, _ in sums:
            mine = ins[first : first + len(parts)]
            first += len(parts)
            if parts[0].ndim == 4:
                for k in (here[CORE], 1 - here[CORE]):
                    out_refs.pop(0)[...] = sum(r[0, k].astype(F32) for r in mine)
            else:
                out_refs.pop(0)[...] = sum(r[0].astype(F32) for r in mine)

    return call(kernel, line, inputs, in_blocks, outs, [None] * len(outs), (1,))


def only_riders(line):
    call(lambda *_: None, line, [], [], [], [], (1,))


def place_columns(line, pairs_of, shapes, moves):
    def kernel(here, *refs):
        ins, outs = refs[: 2 * len(pairs_of)], refs[2 * len(pairs_of) :]
        c = here[CORE]
        for pair, first, wide, out, column0, column1 in moves:
            for turn in range(2):
                k = c if turn == 0 else 1 - c
                to = pl.multiple_of(column0 + k * (column1 - column0), wide)
                outs[out][:, pl.ds(to, wide)] = ins[2 * pair + turn][:, first : first + wide]

    inputs = [a for pair in pairs_of for a in pair]
    return call(
        kernel,
        line,
        inputs,
        [None] * len(inputs),
        [sds(s, F32) for s in shapes],
        [None] * len(shapes),
        (1,),
    )


def back_through(line, back, weight):
    rows, hidden = back.shape
    width = weight.shape[0]
    wide = 512

    def kernel(here, back_ref, w_ref, out_ref):
        out_ref[...] = dot(back_ref[...], w_ref[...], 1, 1).astype(BF16)

    return call(
        kernel,
        line,
        [back, weight],
        [None, ((wide, hidden), lambda n, c: (n, 0))],
        [sds((rows, width), BF16)],
        [((rows, wide), lambda n, c: (0, n))],
        (width // wide,),
        flops=2 * rows * hidden * width,
    )[0]


def project_down(line, active, weight, block):
    rows, hidden = active.shape
    width = weight.shape[1]
    half, wide = rows // 2, 512
    view = weight.reshape(hidden // block, 2, block, width)

    def kernel(here, active_ref, w_ref, own_ref, gone_ref):
        def part(which):
            place = pl.ds(pl.multiple_of(which * half, half), half)
            return dot(active_ref[place, :], w_ref[...].reshape(hidden, wide))

        gone_ref[...] = part(1 - here[CORE]).astype(BF16)
        own_ref[...] = part(here[CORE])

    by_cols = ((half, wide), lambda n, c: (0, n))
    return call(
        kernel,
        line,
        [active, view],
        [None, ((hidden // block, None, block, wide), lambda n, c: (0, c[CORE], 0, n))],
        [sds((half, width), F32), sds((half, width), BF16)],
        [by_cols, by_cols],
        (width // wide,),
        flops=2 * rows * hidden * width,
    )


def back_to_attended(line, grad_mine, grad_theirs, mid, cot, gain, weight):
    rows, width = mid.shape
    tall, part = 256, width // 2

    def kernel(here, gm_ref, gt_ref, mid_ref, cot_ref, gain_ref, w_ref, out_ref, cols_ref, mg_ref, gain_grad_ref):
        c = here[CORE]
        incoming = gm_ref[...].astype(F32) + gt_ref[...].astype(F32)
        centred, scale = moments(mid_ref[...])
        x_hat = centred * scale
        terms = incoming * x_hat
        scaled = incoming * gain_ref[...]
        mean_a = jnp.mean(scaled, axis=-1, keepdims=True)
        mean_b = jnp.mean(terms * gain_ref[...], axis=-1, keepdims=True)
        mid_grad = cot_ref[...].astype(F32) + scale * (scaled - mean_a - x_hat * mean_b)
        mg_ref[...] = mid_grad
        branch = mid_grad.astype(BF16)
        out_ref[...] = dot(branch, w_ref[pl.ds(pl.multiple_of(c * part, part), part), :], 1, 1).astype(BF16)
        cols_ref[...] = jnp.where(c == 0, branch[:, :part], branch[:, part:])

        @pl.when(pl.program_id(0) == 0)
        def _():
            gain_grad_ref[...] = jnp.zeros_like(gain_grad_ref)

        gain_grad_ref[...] += jnp.sum(terms.reshape(tall // 8, 8, width), axis=0)

    by_rows = ((tall, width), lambda i, c: (i, 0))
    half_rows = ((tall, part), lambda i, c: (i, 0))
    return call(
        kernel,
        line,
        [grad_mine, grad_theirs, mid, cot, gain, weight],
        [by_rows, by_rows, by_rows, by_rows, None, None],
        [
            sds((rows, part), BF16),
            sds((rows, part), BF16),
            sds((rows, width), F32),
            sds((8, width), F32),
        ],
        [half_rows, half_rows, by_rows, None],
        (rows // tall,),
        flops=rows * width * width,
    )


def back_through_qkv(line, backs, weight):
    rows = backs[0].shape[0]
    width, columns = weight.shape
    half, wide = rows // 2, 512

    def kernel(here, *refs):
        back_refs, (w_ref, own_ref, gone_ref) = refs[: len(backs)], refs[len(backs) :]

        def some(which):
            place = pl.ds(pl.multiple_of(which * half, half), half)
            total, first = 0.0, 0
            for ref in back_refs:
                last = first + ref.shape[1]
                total = total + dot(ref[place, :], w_ref[:, first:last], 1, 1)
                first = last
            return total

        gone_ref[...] = some(1 - here[CORE]).astype(BF16)
        own_ref[...] = some(here[CORE])

    by_cols = ((half, wide), lambda n, c: (0, n))
    return call(
        kernel,
        line,
        [*backs, weight],
        [*[None] * len(backs), ((wide, columns), lambda n, c: (n, 0))],
        [sds((half, width), F32), sds((half, width), BF16)],
        [by_cols, by_cols],
        (width // wide,),
        flops=2 * rows * columns * width,
    )


def back_to_tokens(line, grad_own, grad_came, toks, pass_embed, gain, mid_grad):
    half, width = grad_own.shape
    tall = 256
    steps = half // tall

    def kernel(here, own_ref, came_ref, toks_ref, pass_ref, gain_ref, mg_ref, out_ref, sums_ref):
        incoming = own_ref[...] + came_ref[...].astype(F32)
        centred, scale = moments(toks_ref[...].astype(F32) + pass_ref[...])
        x_hat = centred * scale
        terms = incoming * x_hat
        scaled = incoming * gain_ref[...]
        mean_a = jnp.mean(scaled, axis=-1, keepdims=True)
        mean_b = jnp.mean(terms * gain_ref[...], axis=-1, keepdims=True)
        resid_grad = mg_ref[...] + scale * (scaled - mean_a - x_hat * mean_b)
        out_ref[...] = resid_grad.astype(BF16)

        @pl.when(pl.program_id(0) == 0)
        def _():
            sums_ref[...] = jnp.zeros_like(sums_ref)

        sums_ref[0] += jnp.sum(resid_grad.reshape(tall // 8, 8, width), axis=0)
        sums_ref[1] += jnp.sum(terms.reshape(tall // 8, 8, width), axis=0)

    by_rows = ((tall, width), lambda i, c: (i, 0))
    own_rows = ((tall, width), lambda i, c: (c[CORE] * steps + i, 0))
    return call(
        kernel,
        line,
        [grad_own, grad_came, toks, pass_embed, gain, mid_grad],
        [by_rows, by_rows, own_rows, None, None, own_rows],
        [sds((half, width), BF16), sds((2, 8, width), F32)],
        [by_rows, None],
        (steps,),
        flops=20 * half * width,
    )


def body(
    sizes,
    tokens,
    seq_lengths,
    pass_embed,
    norm1_gain,
    qkv_weight,
    out_weight,
    norm2_gain,
    up_weight,
    down_weight,
    cotangent,
):
    n_chip, n_core, n_half, n_lane = sizes
    n_head = n_half * n_lane
    tok_rows, width = tokens.shape
    rows = 2 * tok_rows
    group_rows = tok_rows * n_head
    hidden = up_weight.shape[1]
    core = lax.axis_index("core")
    chip = lax.axis_index("chip")
    half = lax.axis_index("half")
    head = half * n_lane + lax.axis_index("lane")
    pass_row, gain1, gain2 = (v.reshape(1, width) for v in (pass_embed, norm1_gain, norm2_gain))

    def index(c, k, h, l):
        return ((c * n_core + k) * n_half + h) * n_lane + l

    everyone = [
        (c, k, h, l)
        for c in range(n_chip)
        for k in range(n_core)
        for h in range(n_half)
        for l in range(n_lane)
    ]
    def across_chip(pick):
        return [
            (index(c, k, h, l), index(c, 1 - k, h, l)) for c, k, h, l in everyone if pick(k, h)
        ]

    def stay(k, h):
        return k == h

    def leave(k, h):
        return k != h

    leavers = [d for d in everyone if leave(d[1], d[2])]
    regroup_perm = [(index(c, k, h, l), index(c, h, k, l)) for c, k, h, l in leavers]
    beside_perm = [(index(c, k, h, l), index(c, k, 1 - h, l)) for c, k, h, l in leavers]

    def send(value, pairs):
        return lax.ppermute(value, AXES, pairs)

    def regroup(value):
        return jnp.where(core == half, value, send(value, regroup_perm))

    def across(value):
        return lax.ppermute(value, "core", [(0, 1), (1, 0)])

    n_chips = n_chip * n_head
    n_bits = n_chips.bit_length() - 1
    number = chip * n_head + head
    bits = list(range(n_bits))
    near = ([0, 1, *bits[2:]], [1, 0, *bits[2:]])
    far_first = ([*bits[2:], 0, 1], [*bits[2:], 1, 0])

    tables, length = {}, 0

    def device_numbers(c, k, h, l):
        nonlocal length
        found = [k, h, int(k == h), 1 - h]
        me = c * n_head + h * n_lane + l
        for name, orders in (("near", near), ("far", far_first)):
            order = orders[k]
            mine = [(me >> b) & 1 for b in order]

            def pack(values):
                value = 0
                for v in values:
                    value = value * 2 + v
                return value

            def chip_at(place):
                values = [(place >> (n_bits - 1 - s)) & 1 for s in range(n_bits)]
                values[0] = mine[0] if values[0] else 1 - mine[0]
                return sum(v << b for v, b in zip(values, order))

            sources = [chip_at(p) for p in range(n_chips)]
            tables[name, "sources"] = len(found)
            found += sources
            tables[name, "places"] = len(found)
            found += [sources.index(n) for n in range(n_chips)]
            for step in range(1, n_bits):
                tables[name, step] = len(found)
                wanted = [*mine[:step], 1 - mine[step]]
                found += [pack(wanted[max(p, 1) :]) for p in range(step + 1)]
            tables[name, "last"] = len(found)
            found += [pack(mine[max(p, 1) :]) for p in range(n_bits + 1)]
        length = len(found)
        return found

    table = jnp.asarray([device_numbers(*d) for d in everyone], jnp.int32)
    here = lax.dynamic_slice(table, (lax.axis_index(AXES), 0), (1, length))[0]
    line = {"here": here, "turn": [], "sums": {}, "rides": {}, "after": [], "count": 0, "cost": COSTS}

    def flip(orders, step):
        def partner(c, k, h, l):
            other = (c * n_head + h * n_lane + l) ^ (1 << orders[k][step])
            return index(other // n_head, k, other % n_head // n_lane, other % n_lane)

        return [(index(*d), partner(*d)) for d in everyone]

    def sum_over_chips(name, gone, kept):
        orders = near if name == "near" else far_first
        parts = [kept]

        def send_blocks(arrays):
            parts.append(lax.ppermute(arrays[0], AXES, flip(orders, len(parts) - 1)))

        def starts():
            first = tables[name, "last" if len(parts) > n_bits else len(parts) - 1]
            return [first + p for p in range(len(parts))]

        def next_step():
            return list(parts), [(starts(), n_chips >> len(parts))]

        def advance():
            count = n_chips >> len(parts)
            send_blocks(
                [
                    sum(
                        lax.dynamic_slice_in_dim(p, here[at] * count, count, 0).astype(F32)
                        for p, at in zip(parts, starts())
                    ).astype(BF16)
                ]
            )

        def finish():
            while len(parts) <= n_bits:
                advance()
            return list(parts), starts()

        send_blocks([gone])
        return {"next_step": next_step, "send": send_blocks, "finish": finish}

    def split(whole, orders):
        view = whole.reshape((2,) * n_bits + whole.shape[1:])
        tail = tuple(range(n_bits, view.ndim))
        turned = [
            jnp.transpose(view, tuple(n_bits - 1 - b for b in o) + tail) for o in orders
        ]
        at = jnp.where(core == 0, (number >> orders[0][0]) & 1, (number >> orders[1][0]) & 1)

        def take(where):
            found = [lax.dynamic_index_in_dim(t, where, 0, keepdims=False) for t in turned]
            return jnp.where(core == 0, *found).reshape((n_chips // 2,) + whole.shape[1:])

        return take(1 - at), take(at)

    per = width // (n_chips * n_core)

    def gradient(name, *tasks):
        if per % 16 == 0:
            return rows_gradient(
                line, tables[name, "sources"], tasks, n_chips, n_core, n_head
            )
        wholes = []
        for lefts, right in tasks:
            left = lefts[0]
            if len(lefts) == 2:
                left = jnp.where(
                    core == 0, jnp.concatenate(lefts, axis=1), jnp.concatenate(lefts[::-1], axis=1)
                )
            wholes.append(rows_gradient_whole(line, left, right))
        whole = jnp.concatenate(wholes, axis=1)
        view = whole.reshape(n_chip, n_core, n_head, per, whole.shape[1])
        return split(jnp.swapaxes(view, 1, 2).reshape(n_chips, n_core, per, -1), near)

    part = width // 2
    ff_block = hidden // (n_chip * n_core)
    core_pairs = part // (2 * HEAD_DIM)
    stays = (core == half).astype(jnp.int32)

    def spread_group(value):
        near_came = send(value, across_chip(stay))
        leaver_came, stayer_came = send(value, regroup_perm), send(value, beside_perm)
        return [(value, near_came, (0, 0))], [(stayer_came, leaver_came, (1, 0))]

    near_toks, far_toks = spread_group(tokens)
    lengths_came = send(seq_lengths, across_chip(stay))
    qkv_here = qkv_columns(line, qkv_weight)
    first_half = project_qkv(
        line, HALF, [p[:2] for p in near_toks], pass_row, gain1, qkv_here
    )
    up_here = up_columns(line, up_weight, ff_block)
    near_cot, far_cot = spread_group(cotangent)
    toks, normed_a, qkv = project_qkv(
        line, OTHER_HALF, [p[:2] for p in far_toks], pass_row, gain1, qkv_here, first_half
    )
    lengths = jnp.where(core == half, seq_lengths, lengths_came)[0]
    order = jnp.arange(lengths.shape[0])
    ends = jnp.sum(jnp.where(order[:, None] <= order[None, :], lengths[:, None], 0), axis=0)

    def to_heads(value):
        value = lax.all_to_all(value, "lane", split_axis=1, concat_axis=0, tiled=True)
        value = value.reshape(n_lane, 2, tok_rows, -1)
        return jnp.swapaxes(value, 0, 1).reshape(group_rows, -1)

    def from_heads(value):
        value = value.reshape(2, n_lane, tok_rows, -1)
        value = jnp.swapaxes(value, 0, 1).reshape(group_rows, -1)
        return lax.all_to_all(value, "lane", split_axis=0, concat_axis=1, tiled=True)

    if n_lane > 1:
        qkv = to_heads(qkv)
    pairs = core_pairs // n_lane
    attended_heads, totals = attend(line, ends, qkv)
    mine = from_heads(attended_heads) if n_lane > 1 else attended_heads
    theirs = across(mine)

    line["after"] += [p for pair in far_cot for p in pair[:2]]
    middle, normed_m = project_out(
        line, mine, theirs, toks, pass_row, out_weight, gain2
    )
    per_ff = hidden // 2 // n_chips
    down_orders, cuts = ["near"], [per_ff]
    if per_ff % 32 == 0 and n_bits > 3:
        down_orders, cuts = ["far", "near"], [per_ff // 2] * 2
    active, upper_grad, cot, piles = feed_forward(
        line,
        [tables[name, "places"] for name in down_orders],
        normed_m,
        [*near_cot, *far_cot],
        up_here,
        down_weight,
        ff_block,
        n_chips,
        cuts,
    )
    down_sums = [sum_over_chips(o, *pile) for o, pile in zip(down_orders, piles)]
    normed_m_part = back_through(line, upper_grad, up_here)
    normed_m_came = across(normed_m_part)
    up_sum = sum_over_chips("near", *gradient("near", ([normed_m], upper_grad)))
    half_pairs = pairs if n_lane > 1 else max(1, pairs // 2)
    several = half_pairs < pairs and len(down_sums) > 1
    if several:
        line["rides"] = RIDES
        line["sums"] = {"a": down_sums[0], "b": down_sums[1], "u": up_sum}

    attended_grad, branch_cols, middle_grad, norm2_terms = back_to_attended(
        line, normed_m_part, normed_m_came, middle, cot, gain2, out_weight
    )
    if n_lane > 1:
        attended_grad = to_heads(attended_grad)

    def back_pairs(first):
        back = attend_back(
            line, ends, qkv, attended_heads, attended_grad, totals, first, half_pairs
        )
        return from_heads(back) if n_lane > 1 else back

    backs = [back_pairs(0)]
    rest_sums = [
        sum_over_chips("near",
            *gradient("near", ([normed_a], backs[0]), ([mine, theirs], branch_cols)),
        )
    ]
    line["sums"]["r"] = rest_sums[0]
    if half_pairs < pairs:
        backs.append(back_pairs(half_pairs))
        rest_sums.append(sum_over_chips("near", *gradient("near", ([normed_a], backs[1]))))
        line["sums"]["s"] = rest_sums[1]
    normed_a_own, normed_a_gone = back_through_qkv(line, backs, qkv_here)
    normed_a_came = across(normed_a_gone)
    output_own, output_gone = project_down(line, active, down_weight, ff_block)
    output_came = across(output_gone)
    token_grad, sums = back_to_tokens(
        line, normed_a_own, normed_a_came, toks, pass_row, gain1, middle_grad
    )
    token_grad = regroup(token_grad)
    if several:
        only_riders(line)
        only_riders(line)
    middle_own = lax.dynamic_slice_in_dim(middle, core * tok_rows, tok_rows, 0)
    mixed = regroup((middle_own + output_own + output_came.astype(F32)).astype(BF16))

    down_grad = jnp.concatenate(
        last_sums(line, [s["finish"]() for s in down_sums]), axis=0
    )
    up_own, up_gone = last_sums(line, [up_sum["finish"]()])
    up_pair = (up_own, across(up_gone))
    (up_grad,) = place_columns(
        line,
        [up_pair],
        [(per, hidden)],
        [
            (0, n * ff_block, ff_block, 0, 2 * n * ff_block, (2 * n + 1) * ff_block)
            for n in range(n_chip)
        ],
    )
    small = jnp.sum(jnp.concatenate([sums, 0.5 * norm2_terms[None]]), axis=1) + up_grad[:1, :1] * 0
    n_all = len(everyone)
    small = jnp.swapaxes(small.reshape(3, n_all, width // n_all), 0, 1)
    small = lax.all_to_all(small, AXES, split_axis=0, concat_axis=0, tiled=True)
    small = jnp.sum(small, axis=0)
    rest = last_sums(line, [s["finish"]() for s in rest_sums])
    pairs_of = [(rest[2 * n], across(rest[2 * n + 1])) for n in range(len(rest_sums))]
    size = 3 * part // len(rest_sums)
    moves = [(0, size, part, 0, 0, part)]
    two = 2 * HEAD_DIM
    for n in range(3):
        for lane in range(n_lane):
            for r in range(len(rest_sums)):
                for p in range(half_pairs):
                    first = ((lane * half_pairs + p) * 3 + n) * two
                    column = n * width + (lane * pairs + r * half_pairs + p) * two
                    moves.append((r, first, two, 1, column, column + part))
    line["after"] = [small]
    out_grad, qkv_grad = place_columns(
        line, pairs_of, [(per, width), (per, 3 * width)], moves
    )

    return (
        mixed,
        token_grad,
        small[0],
        small[1],
        qkv_grad,
        out_grad,
        small[2],
        up_grad,
        down_grad,
    )


def solution(mesh):
    n_dp, n_head = mesh.shape["dp"], mesh.shape["head"]
    sizes = (n_dp // 2, 2, 2, n_head // 2)
    fine = Mesh(mesh.devices.reshape(sizes), AXES)
    rows, group = P(AXES), P(("chip", "core"))
    in_specs = (rows, group, P(), P(), P(), P(), P(), P(), P(), rows)
    return jax.shard_map(
        partial(body, sizes),
        mesh=fine,
        in_specs=in_specs,
        out_specs=(rows,) * 9,
        check_vma=False,
    )
```
